256 devices in a mesh: lat: 32 (over y_lo, z, core), lon: 8 (over y_hi, x).
Axes of the slice: x: 4, y: 4 (y_hi: 2, y_lo: 2; y = y_hi * 2 + y_lo), z: 8, core: 2. Of those that a mesh axis runs over, the one named last changes fastest.
Arguments:
- cotangent: bfloat16 [384, 384, 1024], P(None, 'lat', 'lon'), may hold values from -6 to 6
- layer_input: bfloat16 [384, 384, 1024], P(None, 'lat', 'lon'), may hold values from -6 to 6
- filter_values: bfloat16 [3, 384, 4, 17], replicated, may hold values from -4 to 4
- weights: bfloat16 [3, 384, 384], replicated, may hold values from -0.1875 to 0.1875
- row_offset: int32 [384], replicated, may hold values from -3 to 0, as said below
- reach: int32 [384], replicated, may hold values from 1 to 9, as said below
Outputs:
- input_grad: bfloat16 [384, 384, 1024], P(None, 'lat', 'lon')
- weight_grad: float32 [3, 384, 384], replicated
The draws below stay inside these ranges and needn't reach their ends.
Inputs may be any that keep to these rules, and one draw needn't show every extreme that they name: The support rows of output latitude o are o + row_offset[o] to o + row_offset[o] + 3. Taps d with |d| < reach[o] are used.
All inputs are finite; a program needn't handle non-finite values.
Results may differ from the reference program's by a relative error of at most 0.0049.
Values may be sent and summed in bfloat16 or wider, within the bound.
A program may use at most 128 MiB of HBM per device.

```python
import math
import jax
import jax.numpy as jnp
from jax import lax

C = 384
K = 3
S = 4
Q = 8
TAPS = 17
NLAT = 384
NLON = 1024


def draw_row_offset(key, part):
    values = jax.random.randint(jax.random.fold_in(key, 11), (NLAT,), -(S - 1), 1)
    values = values.at[0].set(-(S - 1)).at[NLAT - 1].set(0)
    return values.astype(jnp.int32)


def draw_reach(key, part):
    rows = jnp.arange(NLAT, dtype=jnp.int32)
    dist = jnp.minimum(rows, NLAT - 1 - rows)
    base = Q + 1 - Q * 4 * dist // NLAT
    jitter = jax.random.randint(jax.random.fold_in(key, 23), (NLAT,), -1, 2)
    values = jnp.clip(base + jitter, 1, Q + 1)
    values = values.at[0].set(Q + 1).at[NLAT // 2].set(1)
    return values.astype(jnp.int32)


def steps_of(rng, dims, cuts, smallest, largest):
    loudness = 1.0
    for position, parts in cuts:
        draws = jax.random.uniform(jax.random.fold_in(jax.random.fold_in(rng, 6), position), (parts,), jnp.float32, smallest / len(cuts), largest / len(cuts))
        loudness = loudness * jnp.repeat(jnp.exp(draws), dims[position] // parts).reshape((-1,) + (1,) * (len(dims) - 1 - position))
    return loudness


def gaussian(own_key, shape, deviation, most, shards=(), held_as=jnp.bfloat16):
    drawn = jax.random.normal(own_key, shape, jnp.float32) * deviation
    if len(shards) > 0:
        drawn = steps_of(own_key, shape, shards, -0.22, 0.18) * drawn
    return jnp.clip(drawn, min=-most, max=most).astype(held_as)


def setup_inputs(seed: int = 0) -> dict:
    arg_keys = jax.random.split(jax.random.key(seed), 7)
    cotangent = gaussian(arg_keys[0], (C, NLAT, NLON), 1.0, 6.0, ((1, 32), (2, 8)))
    layer_input = gaussian(arg_keys[1], (C, NLAT, NLON), 1.0, 6.0, ((1, 32), (2, 8)))
    filter_values = gaussian(arg_keys[2], (K, NLAT, S, TAPS), 0.3, 4.0)
    weights = gaussian(arg_keys[3], (K, C, C), (K * C) ** -0.5, 0.1875)
    row_offset = draw_row_offset(jax.random.fold_in(arg_keys[6], 71), 0)
    reach = draw_reach(jax.random.fold_in(arg_keys[6], 71), 0)
    return {"cotangent": cotangent, "layer_input": layer_input, "filter_values": filter_values, "weights": weights, "row_offset": row_offset, "reach": reach}


def shift_rows(field, delta):
    count = field.shape[2]
    if delta == 0:
        return field
    if delta > 0:
        pad = jnp.zeros(field.shape[:2] + (delta,) + field.shape[3:], jnp.float32)
        return jnp.concatenate([pad, field[:, :, :count - delta]], axis=2)
    pad = jnp.zeros(field.shape[:2] + (-delta,) + field.shape[3:], jnp.float32)
    return jnp.concatenate([field[:, :, -delta:], pad], axis=2)

def reference(cotangent, layer_input, filter_values, weights, row_offset, reach):
    kernels, nlat, span, taps = filter_values.shape
    reach_q = (taps - 1) // 2
    feature_channels, _, nlon = cotangent.shape
    tap_ids = jnp.arange(taps, dtype=jnp.int32) - reach_q
    live = (jnp.abs(tap_ids)[None, :] < reach[:, None]).astype(jnp.float32)
    psi = filter_values.astype(jnp.float32) * live[None, :, None, :]
    deltas = jnp.arange(2 * span - 1, dtype=jnp.int32) - (span - 1)
    level = deltas[None, :] - row_offset[:, None]
    pick = (level[:, :, None] == jnp.arange(span, dtype=jnp.int32)[None, None, :]).astype(jnp.float32)
    coeff = jnp.einsum('ods,kost->kodt', pick, psi)
    block = math.gcd(feature_channels, 32)
    blocks = feature_channels // block
    gy_blocks = cotangent.reshape(blocks, block, nlat, nlon)
    w_blocks = weights.reshape(kernels, blocks, block, feature_channels).transpose(1, 0, 2, 3)
    gathered_input = layer_input.astype(jnp.float32)

    def step(gradient_accumulator, pair):
        gy_b, weight_per_block = pair
        gyf = gy_b.astype(jnp.float32)
        rolled = jnp.stack([jnp.roll(gyf, t - reach_q, axis=2) for t in range(taps)])
        tap_spread_width = jnp.zeros((kernels, block, nlat, nlon), jnp.float32)
        for di in range(2 * span - 1):
            value = jnp.einsum('kot,tcol->kcol', coeff[:, :, di, :], rolled)
            tap_spread_width = tap_spread_width + shift_rows(value, di - (span - 1))
        tap_spread_width = tap_spread_width.astype(jnp.bfloat16).astype(jnp.float32)
        gradient_accumulator = gradient_accumulator + jnp.einsum('ygv,ygtj->vtj', weight_per_block.astype(jnp.float32), tap_spread_width)
        filter_weight_gradient = jnp.einsum('enyw,jyw->enj', tap_spread_width, gathered_input)
        return (gradient_accumulator, filter_weight_gradient)
    gradient_accumulator, wparts = lax.scan(step, jnp.zeros((feature_channels, nlat, nlon), jnp.float32), (gy_blocks, w_blocks))
    weight_grad = wparts.transpose(1, 0, 2, 3).reshape(kernels, feature_channels, feature_channels)
    weight_grad = weight_grad / jnp.sqrt(jnp.float32(nlat * nlon))
    return (gradient_accumulator.astype(jnp.bfloat16), weight_grad)
```

```python
import functools

import jax
import jax.numpy as jnp
from jax import lax
from jax.experimental import pallas as pl
from jax.experimental.pallas import tpu as pltpu
from jax.sharding import PartitionSpec as P

MESH = pl.DeviceIdType.MESH
F32 = jnp.float32
BF16 = jnp.bfloat16


def iota(shape, dim):
    return lax.broadcasted_iota(jnp.int32, shape, dim)


def ceil_to(n, m):
    return -(-n // m) * m


class Plan:
    def __init__(self, lat, lon, channels, rows, cols, nlat, kernels, span, taps):
        self.lat, self.lon = lat, lon
        self.c, self.rows, self.cols = channels, rows, cols
        self.nlat, self.k, self.span, self.taps = nlat, kernels, span, taps
        self.q = (taps - 1) // 2
        self.rim = span - 1
        self.tall = rows + 2 * self.rim
        self.near = 2 * span - 1
        self.pairs = rows // 2
        self.z = lat // 4
        self.xy = 2 * lon
        self.mix = kernels * channels
        self.chunk = self.mix // 6
        self.blocks = channels // 128
        self.part = self.chunk * self.blocks
        self.half = 3 * self.part
        self.piece = ceil_to(-(-self.half // self.xy), 16)
        self.sub = ceil_to(-(-self.piece // self.z), 16)
        self.window = self.near + 1
        self.band = self.window * cols
        self.deep = self.band + self.window * 16


def remote(src, dst, sems, n, device):
    return pltpu.make_async_remote_copy(
        src_ref=src,
        dst_ref=dst,
        send_sem=sems[0].at[n],
        recv_sem=sems[1].at[n],
        device_id=device,
        device_id_type=MESH,
    )


def kernel(
    g,
    cot,
    xin,
    w_in,
    fv,
    ro,
    reach,
    out,
    gathered,
    cot_s,
    x_s,
    xt,
    w_s,
    wt,
    taps_s,
    toep,
    sp,
    pack_l,
    pack_r,
    left,
    right,
    rim_s,
    grad,
    core_in,
    grad16,
    xy_in,
    own,
    z_in,
    sub16,
    own16,
    out_s,
    local_sem,
    halo_send,
    halo_recv,
    core_send,
    core_recv,
    xy_send,
    xy_recv,
    z_send,
    z_recv,
    zg_send,
    zg_recv,
    xyg_send,
    xyg_recv,
):
    lat = lax.axis_index("lat")
    lon = lax.axis_index("lon")
    core = lax.rem(lat, 2)
    zi = lax.rem(lat // 2, g.z)
    ylo = lat // (2 * g.z)
    me_xy = ylo * g.lon + lon
    up, down = lax.rem(lat + 1, g.lat), lax.rem(lat + g.lat - 1, g.lat)
    east, west = lax.rem(lon + 1, g.lon), lax.rem(lon + g.lon - 1, g.lon)
    sibling = (lat + 1 - 2 * core, lon)

    def xy_peer(d):
        peer = lax.rem(me_xy + d, g.xy)
        return peer, ((peer // g.lon) * (2 * g.z) + lax.rem(lat, 2 * g.z), lax.rem(peer, g.lon))

    def z_peer(d):
        peer = lax.rem(zi + d, g.z)
        return peer, (ylo * 2 * g.z + peer * 2 + core, lon)

    halo = [
        (up, lon),
        (down, lon),
        (lat, east),
        (lat, west),
        (up, east),
        (up, west),
        (down, east),
        (down, west),
    ]
    partners = halo + [sibling]
    partners += [xy_peer(d)[1] for d in range(1, g.xy)]
    partners += [z_peer(d)[1] for d in range(1, g.z)]

    barrier = pltpu.get_barrier_semaphore()
    for peer in partners:
        pl.semaphore_signal(barrier, inc=1, device_id=peer, device_id_type=MESH)

    load_cot = pltpu.make_async_copy(cot, cot_s.at[pl.ds(g.rim, g.rows)], local_sem.at[0])
    load_x = pltpu.make_async_copy(xin, x_s, local_sem.at[1])
    load_w = pltpu.make_async_copy(w_in, w_s, local_sem.at[2])
    load_cot.start()
    load_x.start()
    load_w.start()
    load_cot.wait()

    pick = iota((16, g.cols), 0)
    lane = iota((16, g.cols), 1)
    pick = (lane == jnp.where(pick < 8, pick + (g.cols - 8), pick - 8)).astype(F32).astype(BF16)
    for o in range(0, g.rows, 2):
        edge = [
            lax.dot_general(
                pick, cot_s[g.rim + o + n], (((1,), (1,)), ((), ())), preferred_element_type=F32
            )
            for n in range(2)
        ]
        pack_r[8 * o : 8 * o + 16, :] = jnp.concatenate([edge[0][:8], edge[1][:8]], 0).astype(BF16)
        pack_l[8 * o : 8 * o + 16, :] = jnp.concatenate([edge[0][8:], edge[1][8:]], 0).astype(BF16)

    pl.semaphore_wait(barrier, len(partners))

    sems = (halo_send, halo_recv)
    n_own = 8 * g.rows
    last = n_own - 32
    rim, tall, rows = g.rim, g.tall, g.rows
    sends = [
        remote(cot.at[pl.ds(rows - rim, rim)], cot_s.at[pl.ds(0, rim)], sems, 0, halo[0]),
        remote(cot.at[pl.ds(0, rim)], cot_s.at[pl.ds(tall - rim, rim)], sems, 1, halo[1]),
        remote(pack_r, left.at[pl.ds(32, n_own)], sems, 2, halo[2]),
        remote(pack_l, right.at[pl.ds(32, n_own)], sems, 3, halo[3]),
        remote(pack_r.at[pl.ds(last, 32)], left.at[pl.ds(0, 32)], sems, 4, halo[4]),
        remote(pack_l.at[pl.ds(last, 32)], right.at[pl.ds(0, 32)], sems, 5, halo[5]),
        remote(pack_r.at[pl.ds(0, 32)], left.at[pl.ds(32 + n_own, 32)], sems, 6, halo[6]),
        remote(pack_l.at[pl.ds(0, 32)], right.at[pl.ds(32 + n_own, 32)], sems, 7, halo[7]),
    ]
    for copy in sends:
        copy.start()

    source = iota((32, g.nlat), 1)
    slot = iota((32, g.nlat), 0)
    here = (source == lat * rows - rim + slot) & (slot < tall)
    moved = lax.dot_general(
        here.astype(F32).astype(BF16), fv[...], (((1,), (1,)), ((), ())), preferred_element_type=F32
    )
    first = jnp.sum(jnp.where(here, ro[...].astype(F32), 0.0), axis=1, keepdims=True).astype(jnp.int32)
    reached = jnp.sum(jnp.where(here, reach[...].astype(F32), 0.0), axis=1, keepdims=True)
    reached = reached.astype(jnp.int32)
    column = iota((32, 256), 1)
    level = column & 3
    order = column >> 2
    tap = order
    for n in range(1, g.k):
        tap = tap - jnp.where(order >= n * g.taps, g.taps, 0)
    moved = jnp.where(jnp.abs(tap - g.q) < reached, moved, 0.0)
    levels = jnp.concatenate(
        [jnp.where(level == g.rim - j - first, moved, 0.0) for j in range(g.near)], 0
    ).astype(BF16)
    entry = iota((256, g.k * 128), 0) >> 2
    place = iota((256, g.k * 128), 1)
    offset = ((place & 127) + g.q) & 127
    wanted = (place >> 7) * g.taps + offset
    spot = ((entry == wanted) & (offset < g.taps)).astype(F32).astype(BF16)
    placed = jnp.dot(levels, spot, preferred_element_type=F32)
    for k in range(g.k):
        taps_s[k] = placed[:, k * 128 : (k + 1) * 128]

    l_in = iota((g.cols, g.cols), 0)
    l_out = iota((g.cols, g.cols), 1)
    near = jnp.abs(l_in - l_out) <= g.q
    m_in = iota((8, g.cols), 0)
    m_out = iota((8, g.cols), 1)
    from_left = m_out <= m_in
    from_right = m_out >= m_in + (g.cols - 8)

    def build(p, carry):
        for i in range(2):
            empty = (g.window - 1) * (1 - i)
            for k in range(g.k):
                lanes = slice((2 * k + i) * 128, (2 * k + i + 1) * 128)
                toep[p, empty * 128 : (empty + 1) * 128, lanes] = jnp.zeros((128, 128), BF16)
                rim_row = g.band + empty * 16
                toep[p, rim_row : rim_row + 16, lanes] = jnp.zeros((16, 128), BF16)
                for j in range(g.near):
                    row = taps_s[k, pl.ds(j * 32 + 2 * p + i + j, 1), :]
                    wheel = pltpu.roll(
                        jnp.broadcast_to(row, (128, 128)), 0, 1, stride=1, stride_axis=0
                    )
                    at = i + j
                    toep[p, at * 128 : (at + 1) * 128, lanes] = jnp.where(near, wheel, 0.0).astype(BF16)
                    corner = jnp.concatenate(
                        [
                            jnp.where(from_left, wheel[120:], 0.0),
                            jnp.where(from_right, wheel[:8], 0.0),
                        ],
                        0,
                    )
                    rim_row = g.band + at * 16
                    toep[p, rim_row : rim_row + 16, lanes] = corner.astype(BF16)
        return carry

    lax.fori_loop(0, g.pairs, build, 0)

    load_x.wait()
    load_w.wait()
    for i in range(rows):
        xt[i * 128 : (i + 1) * 128, :] = x_s[i].T
    for k in range(g.k):
        wt[:, k * g.c : (k + 1) * g.c] = w_s[k * g.c : (k + 1) * g.c, :].T

    for copy in sends:
        copy.wait()

    for w in range(tall):
        at = 16 * ((w + 1) // 2)
        odd = 8 * ((w + 1) % 2)
        rim_s[16 * w : 16 * w + 16, :] = jnp.concatenate(
            [
                left[at : at + 16, :].astype(F32)[odd : odd + 8],
                right[at : at + 16, :].astype(F32)[odd : odd + 8],
            ],
            0,
        ).astype(BF16)

    def spread(p, carry):
        wide = [cot_s[2 * p + j] for j in range(g.window)]
        ends = rim_s[pl.ds(pl.multiple_of(32 * p, 32), 16 * g.window), :]
        wide.append(ends.T)
        total = jnp.dot(jnp.concatenate(wide, 1), toep[p], preferred_element_type=F32)
        for k in range(g.k):
            sp[p, k * g.c : (k + 1) * g.c, :] = total[:, k * 256 : (k + 1) * 256].astype(BF16)
        return carry

    lax.fori_loop(0, g.pairs, spread, 0)

    def term(h, n):
        row = pl.multiple_of(h * (3 * g.chunk) + n * g.chunk, 32)
        at = pl.multiple_of(h * g.half + n * g.part, 8)
        rows_of = [sp[p, pl.ds(row, g.chunk), :] for p in range(g.pairs)]
        total = jnp.dot(jnp.concatenate(rows_of, 1), xt[...], preferred_element_type=F32)
        for b in range(g.blocks):
            grad[pl.ds(at + b * g.chunk, g.chunk), :] = total[:, b * 128 : (b + 1) * 128]

    theirs = 1 - core
    to_core = []
    for n in range(3):
        term(theirs, n)
        at = pl.multiple_of(theirs * g.half + n * g.part, 8)
        copy = remote(
            grad.at[pl.ds(at, g.part)],
            core_in.at[pl.ds(n * g.part, g.part)],
            (core_send, core_recv),
            n,
            sibling,
        )
        copy.start()
        to_core.append(copy)
    for n in range(3):
        term(core, n)
    for n in range(3):
        to_core[n].wait()
        at = pl.multiple_of(core * g.half + n * g.part, 8)
        both = grad[pl.ds(at, g.part), :] + core_in[n * g.part : (n + 1) * g.part, :]
        grad16[n * g.part : (n + 1) * g.part, :] = both.astype(BF16)
    spare = g.piece * g.xy - g.half
    if spare:
        grad16[g.half :, :] = jnp.zeros((spare, 128), BF16)

    to_xy = []
    for d in range(1, g.xy):
        peer, device = xy_peer(d)
        copy = remote(
            grad16.at[pl.ds(pl.multiple_of(peer * g.piece, 16), g.piece)],
            xy_in.at[d],
            (xy_send, xy_recv),
            d,
            device,
        )
        copy.start()
        to_xy.append(copy)

    def inward(p, carry):
        total = jnp.dot(wt[...], sp[p], preferred_element_type=F32).astype(BF16)
        out_s[2 * p] = total[:, :128]
        out_s[2 * p + 1] = total[:, 128:]
        return carry

    lax.fori_loop(0, g.pairs, inward, 0)
    store_out = pltpu.make_async_copy(out_s, out, local_sem.at[3])
    store_out.start()

    total = grad16[pl.ds(pl.multiple_of(me_xy * g.piece, 16), g.piece), :].astype(F32)
    for d in range(1, g.xy):
        to_xy[d - 1].wait()
        total = total + xy_in[d].astype(F32)
    own[: g.piece, :] = total
    spare = g.sub * g.z - g.piece
    if spare:
        own[g.piece :, :] = jnp.zeros((spare, 128), F32)

    to_z = []
    for d in range(1, g.z):
        peer, device = z_peer(d)
        copy = remote(
            own.at[pl.ds(pl.multiple_of(peer * g.sub, 16), g.sub)],
            z_in.at[d],
            (z_send, z_recv),
            d,
            device,
        )
        copy.start()
        to_z.append(copy)
    mine = pl.ds(pl.multiple_of(zi * g.sub, 16), g.sub)
    total = own[mine, :]
    for d in range(1, g.z):
        to_z[d - 1].wait()
        total = total + z_in[d]
    sub16[...] = total.astype(BF16)

    to_z = []
    for d in range(1, g.z):
        copy = remote(sub16, own16.at[mine], (zg_send, zg_recv), d, z_peer(d)[1])
        copy.start()
        to_z.append(copy)
    own16[mine, :] = sub16[...]
    for copy in to_z:
        copy.wait()

    to_xy = []
    here = pl.ds(pl.multiple_of(me_xy * g.piece, 16), g.piece)
    for d in range(1, g.xy):
        copy = remote(
            own16.at[pl.ds(0, g.piece)],
            gathered.at[core, here],
            (xyg_send, xyg_recv),
            d,
            xy_peer(d)[1],
        )
        copy.start()
        to_xy.append(copy)
    gathered[core, here, :] = own16[: g.piece, :]
    for copy in to_xy:
        copy.wait()
    swap = remote(gathered.at[core], gathered.at[core], (core_send, core_recv), 3, sibling)
    swap.start()
    swap.wait()
    store_out.wait()


def on_device(cotangent, layer_input, filter_values, weights, row_offset, reach):
    channels, rows, cols = cotangent.shape
    kernels, nlat, span, taps = filter_values.shape
    lat, lon = lax.axis_size("lat"), lax.axis_size("lon")
    g = Plan(lat, lon, channels, rows, cols, nlat, kernels, span, taps)
    entries = kernels * taps * span
    table = filter_values.transpose(0, 3, 2, 1).reshape(entries, nlat)
    table = jnp.pad(table, ((0, 256 - entries), (0, 0)))
    anywhere = pl.BlockSpec(memory_space=pl.ANY)
    vmem = pl.BlockSpec(memory_space=pltpu.VMEM)
    dma = pltpu.SemaphoreType.DMA
    field = (rows, channels, cols)
    out, gathered = pl.pallas_call(
        functools.partial(kernel, g),
        out_shape=(
            jax.ShapeDtypeStruct(field, BF16),
            jax.ShapeDtypeStruct((2, g.piece * g.xy, 128), BF16),
        ),
        in_specs=[anywhere, anywhere, anywhere, vmem, vmem, vmem],
        out_specs=(anywhere, vmem),
        scratch_shapes=[
            pltpu.VMEM((g.tall, channels, cols), BF16),
            pltpu.VMEM(field, BF16),
            pltpu.VMEM((rows * cols, channels), BF16),
            pltpu.VMEM((g.mix, channels), BF16),
            pltpu.VMEM((channels, g.mix), BF16),
            pltpu.VMEM((kernels, g.near * 32, 128), F32),
            pltpu.VMEM((g.pairs, g.deep, kernels * 256), BF16),
            pltpu.VMEM((g.pairs, g.mix, 256), BF16),
            pltpu.VMEM((8 * rows, channels), BF16),
            pltpu.VMEM((8 * rows, channels), BF16),
            pltpu.VMEM((8 * rows + 64, channels), BF16),
            pltpu.VMEM((8 * rows + 64, channels), BF16),
            pltpu.VMEM((16 * g.tall, channels), BF16),
            pltpu.VMEM((2 * g.half, 128), F32),
            pltpu.VMEM((g.half, 128), F32),
            pltpu.VMEM((g.piece * g.xy, 128), BF16),
            pltpu.VMEM((g.xy, g.piece, 128), BF16),
            pltpu.VMEM((g.sub * g.z, 128), F32),
            pltpu.VMEM((g.z, g.sub, 128), F32),
            pltpu.VMEM((g.sub, 128), BF16),
            pltpu.VMEM((g.sub * g.z, 128), BF16),
            pltpu.VMEM(field, BF16),
            dma((4,)),
            dma((8,)),
            dma((8,)),
            dma((4,)),
            dma((4,)),
            dma((g.xy,)),
            dma((g.xy,)),
            dma((g.z,)),
            dma((g.z,)),
            dma((g.z,)),
            dma((g.z,)),
            dma((g.xy,)),
            dma((g.xy,)),
        ],
        compiler_params=pltpu.CompilerParams(
            collective_id=0, has_side_effects=True, vmem_limit_bytes=56 * 2**20
        ),
    )(
        cotangent.transpose(1, 0, 2),
        layer_input.transpose(1, 0, 2),
        weights.reshape(kernels * channels, channels),
        table,
        row_offset.reshape(1, nlat),
        reach.reshape(1, nlat),
    )
    total = gathered[:, : g.half].reshape(6, g.blocks, g.chunk, 128)
    total = total.transpose(0, 2, 1, 3).reshape(kernels, channels, channels).astype(F32)
    weight_grad = total / jnp.sqrt(jnp.float32(nlat * cols * lon))
    return out.transpose(1, 0, 2), weight_grad


def solution(mesh):
    return jax.shard_map(
        on_device,
        mesh=mesh,
        in_specs=(P(None, "lat", "lon"), P(None, "lat", "lon"), P(), P(), P(), P()),
        out_specs=(P(None, "lat", "lon"), P()),
        check_vma=False,
    )
```

```python
import functools
import math

import jax
import jax.numpy as jnp
from jax import lax
from jax.experimental import pallas as pl
from jax.experimental.pallas import tpu as pltpu
from jax.sharding import PartitionSpec as P

MESH = pl.DeviceIdType.MESH
F32 = jnp.float32
BF16 = jnp.bfloat16


def iota(shape, dim):
    return lax.broadcasted_iota(jnp.int32, shape, dim)


def ceil_to(n, m):
    return -(-n // m) * m


class Plan:
    def __init__(self, lat, lon, channels, rows, cols, nlat, kernels, span, taps):
        self.lat, self.lon = lat, lon
        self.c, self.rows, self.cols = channels, rows, cols
        self.nlat, self.k, self.span, self.taps = nlat, kernels, span, taps
        self.q = (taps - 1) // 2
        self.rim = span - 1
        self.tall = rows + 2 * self.rim
        self.near = 2 * span - 1
        self.pairs = rows // 2
        self.window = self.near + 1
        self.band = self.window * cols
        self.deep = self.band + self.window * 16
        self.mix = kernels * channels
        self.scale = 1.0 / math.sqrt(nlat * cols * lon)
        self.z = lat // 4
        self.far = self.z // 2
        self.team = 4 * lon
        self.chunks = 2
        self.wide = channels // self.chunks
        self.slim = self.wide // 2
        self.tier = kernels * self.slim
        self.blocks = channels // 128
        self.half = self.blocks * self.tier
        self.piece = ceil_to(-(-self.half // self.team), 16)
        self.owners = self.half // self.piece
        self.idle = self.team - self.owners


def remote(src, dst, sems, n, device):
    return pltpu.make_async_remote_copy(
        src_ref=src,
        dst_ref=dst,
        send_sem=sems[0].at[n],
        recv_sem=sems[1].at[n],
        device_id=device,
        device_id_type=MESH,
    )


def kernel(
    g,
    cot,
    xin,
    w_in,
    fv,
    ro,
    reach,
    out,
    total_out,
    cot_s,
    x_s,
    xt,
    w_s,
    wt,
    table,
    taps_s,
    toep,
    sp,
    pack_l,
    pack_r,
    left,
    right,
    rim_s,
    rim_t,
    grad,
    core_in,
    grad16,
    team_in,
    far_in,
    final,
    gathered,
    out_s,
    local_sem,
    halo_send,
    halo_recv,
    core_send,
    core_recv,
    team_send,
    team_recv,
    far_send,
    far_recv,
    back_send,
    back_recv,
):
    lat = lax.axis_index("lat")
    lon = lax.axis_index("lon")
    core = lax.rem(lat, 2)
    zi = lax.rem(lat // 2, g.z)
    ylo = lat // (2 * g.z)
    z_lo, z_hi = lax.rem(zi, 2), zi // 2
    me = (ylo * g.lon + lon) * 2 + z_lo
    up, down = lax.rem(lat + 1, g.lat), lax.rem(lat + g.lat - 1, g.lat)
    east, west = lax.rem(lon + 1, g.lon), lax.rem(lon + g.lon - 1, g.lon)
    sibling = (lat + 1 - 2 * core, lon)

    def team_peer(d):
        peer = lax.rem(me + d, g.team)
        column = peer // 2
        z = 2 * z_hi + lax.rem(peer, 2)
        return peer, ((column // g.lon) * (2 * g.z) + 2 * z + core, lax.rem(column, g.lon))

    def far_peer(d):
        z = 2 * lax.rem(z_hi + d, g.far) + z_lo
        return (ylo * 2 * g.z + 2 * z + core, lon)

    halo = [
        (up, east),
        (up, west),
        (down, east),
        (down, west),
        (lat, east),
        (lat, west),
        (up, lon),
        (down, lon),
    ]
    partners = halo + [sibling]
    partners += [team_peer(d)[1] for d in range(1, g.team)]
    partners += [far_peer(d) for d in range(1, g.far)]

    barrier = pltpu.get_barrier_semaphore()
    for peer in partners:
        pl.semaphore_signal(barrier, inc=1, device_id=peer, device_id_type=MESH)

    load_cot = pltpu.make_async_copy(cot, cot_s.at[pl.ds(g.rim, g.rows)], local_sem.at[0])
    load_x = pltpu.make_async_copy(xin, x_s, local_sem.at[1])
    load_w = pltpu.make_async_copy(w_in, w_s, local_sem.at[2])
    load_cot.start()
    load_x.start()
    load_w.start()
    load_cot.wait()

    pick = iota((16, g.cols), 0)
    lane = iota((16, g.cols), 1)
    pick = (lane == jnp.where(pick < 8, pick + (g.cols - 8), pick - 8)).astype(F32).astype(BF16)
    for o in range(0, g.rows, 2):
        edge = [
            lax.dot_general(
                pick, cot_s[g.rim + o + n], (((1,), (1,)), ((), ())), preferred_element_type=F32
            )
            for n in range(2)
        ]
        pack_r[8 * o : 8 * o + 16, :] = jnp.concatenate([edge[0][:8], edge[1][:8]], 0).astype(BF16)
        pack_l[8 * o : 8 * o + 16, :] = jnp.concatenate([edge[0][8:], edge[1][8:]], 0).astype(BF16)

    pl.semaphore_wait(barrier, len(partners))

    sems = (halo_send, halo_recv)
    n_own = 8 * g.rows
    last = n_own - 32
    rim, tall, rows = g.rim, g.tall, g.rows
    sends = [
        remote(pack_r.at[pl.ds(last, 32)], left.at[pl.ds(0, 32)], sems, 0, halo[0]),
        remote(pack_l.at[pl.ds(last, 32)], right.at[pl.ds(0, 32)], sems, 1, halo[1]),
        remote(pack_r.at[pl.ds(0, 32)], left.at[pl.ds(32 + n_own, 32)], sems, 2, halo[2]),
        remote(pack_l.at[pl.ds(0, 32)], right.at[pl.ds(32 + n_own, 32)], sems, 3, halo[3]),
        remote(pack_r, left.at[pl.ds(32, n_own)], sems, 4, halo[4]),
        remote(pack_l, right.at[pl.ds(32, n_own)], sems, 5, halo[5]),
        remote(cot.at[pl.ds(rows - rim, rim)], cot_s.at[pl.ds(0, rim)], sems, 6, halo[6]),
        remote(cot.at[pl.ds(0, rim)], cot_s.at[pl.ds(tall - rim, rim)], sems, 7, halo[7]),
    ]
    for copy in sends:
        copy.start()

    entries = g.k * g.taps * g.span
    for k in range(g.k):
        for t in range(g.taps):
            n = (k * g.taps + t) * g.span
            table[n : n + g.span, :] = fv[k, t].astype(F32)
    table[entries:, :] = jnp.zeros((256 - entries, g.nlat), F32)
    source = iota((32, g.nlat), 1)
    slot = iota((32, g.nlat), 0)
    here = (source == lat * rows - rim + slot) & (slot < tall)
    moved = lax.dot_general(
        here.astype(F32).astype(BF16),
        table[...].astype(BF16),
        (((1,), (1,)), ((), ())),
        preferred_element_type=F32,
    )
    first = jnp.where(here, ro[...].astype(F32)[None, :], 0.0)
    first = jnp.sum(first, axis=1, keepdims=True).astype(jnp.int32)
    reached = jnp.where(here, reach[...].astype(F32)[None, :], 0.0)
    reached = jnp.sum(reached, axis=1, keepdims=True).astype(jnp.int32)
    column = iota((32, 256), 1)
    level = column & 3
    order = column >> 2
    tap = order
    for n in range(1, g.k):
        tap = tap - jnp.where(order >= n * g.taps, g.taps, 0)
    moved = jnp.where(jnp.abs(tap - g.q) < reached, moved, 0.0)
    levels = jnp.concatenate(
        [jnp.where(level == g.rim - j - first, moved, 0.0) for j in range(g.near)], 0
    ).astype(BF16)
    entry = iota((256, g.k * 128), 0) >> 2
    place = iota((256, g.k * 128), 1)
    offset = ((place & 127) + g.q) & 127
    wanted = (place >> 7) * g.taps + offset
    spot = ((entry == wanted) & (offset < g.taps)).astype(F32).astype(BF16)
    placed = jnp.dot(levels, spot, preferred_element_type=F32)
    for k in range(g.k):
        taps_s[k] = placed[:, k * 128 : (k + 1) * 128]

    l_in = iota((g.cols, g.cols), 0)
    l_out = iota((g.cols, g.cols), 1)
    near = jnp.abs(l_in - l_out) <= g.q
    m_in = iota((8, g.cols), 0)
    m_out = iota((8, g.cols), 1)
    from_left = m_out <= m_in
    from_right = m_out >= m_in + (g.cols - 8)

    def build(p, carry):
        for i in range(2):
            empty = (g.window - 1) * (1 - i)
            for k in range(g.k):
                lanes = slice((2 * k + i) * 128, (2 * k + i + 1) * 128)
                toep[p, empty * 128 : (empty + 1) * 128, lanes] = jnp.zeros((128, 128), BF16)
                rim_row = g.band + empty * 16
                toep[p, rim_row : rim_row + 16, lanes] = jnp.zeros((16, 128), BF16)
                for j in range(g.near):
                    row = taps_s[k, pl.ds(j * 32 + 2 * p + i + j, 1), :]
                    wheel = pltpu.roll(
                        jnp.broadcast_to(row, (128, 128)), 0, 1, stride=1, stride_axis=0
                    )
                    at = i + j
                    toep[p, at * 128 : (at + 1) * 128, lanes] = jnp.where(near, wheel, 0.0).astype(BF16)
                    corner = jnp.concatenate(
                        [
                            jnp.where(from_left, wheel[120:], 0.0),
                            jnp.where(from_right, wheel[:8], 0.0),
                        ],
                        0,
                    )
                    rim_row = g.band + at * 16
                    toep[p, rim_row : rim_row + 16, lanes] = corner.astype(BF16)
        return carry

    lax.fori_loop(0, g.pairs, build, 0)

    load_x.wait()
    load_w.wait()
    for i in range(rows):
        xt[i * 128 : (i + 1) * 128, :] = x_s[i].T
    for k in range(g.k):
        wt[:, k * g.c : (k + 1) * g.c] = w_s[k * g.c : (k + 1) * g.c, :].T

    for copy in sends:
        copy.wait()

    for w in range(tall):
        at = 16 * ((w + 1) // 2)
        odd = 8 * ((w + 1) % 2)
        rim_s[16 * w : 16 * w + 16, :] = jnp.concatenate(
            [
                left[at : at + 16, :].astype(F32)[odd : odd + 8],
                right[at : at + 16, :].astype(F32)[odd : odd + 8],
            ],
            0,
        ).astype(BF16)

    def spread(m):
        part = slice(m * g.wide, (m + 1) * g.wide)

        def step(p, carry):
            wide = [cot_s[2 * p + j, part, :] for j in range(g.window)]
            if m == 0:
                ends = rim_s[pl.ds(pl.multiple_of(32 * p, 32), 16 * g.window), :].T
                rim_t[p] = ends
                wide.append(ends[part])
            else:
                wide.append(rim_t[p, part, :])
            total = jnp.dot(jnp.concatenate(wide, 1), toep[p], preferred_element_type=F32)
            for k in range(g.k):
                at = k * g.c + m * g.wide
                sp[p, at : at + g.wide, :] = total[:, k * 256 : (k + 1) * 256].astype(BF16)
            return carry

        lax.fori_loop(0, g.pairs, step, 0)

    def term(m, h):
        tiers = []
        for k in range(g.k):
            at = pl.multiple_of(k * g.c + m * g.wide + h * g.slim, 32)
            tiers.append(
                jnp.concatenate([sp[p, pl.ds(at, g.slim), :] for p in range(g.pairs)], 1)
            )
        return jnp.dot(jnp.concatenate(tiers, 0), xt[...], preferred_element_type=F32)

    to_core = [
        remote(grad.at[m], core_in.at[m], (core_send, core_recv), m, sibling)
        for m in range(g.chunks)
    ]

    def give(m):
        total = term(m, 1 - core)
        for b in range(g.blocks):
            grad[m, b * g.tier : (b + 1) * g.tier, :] = total[:, b * 128 : (b + 1) * 128]
        to_core[m].start()

    def keep(m):
        total = term(m, core)
        to_core[m].wait()
        for b in range(g.blocks):
            at = slice(b * g.tier, (b + 1) * g.tier)
            both = total[:, b * 128 : (b + 1) * 128] + core_in[m, at, :]
            grad16[m, at, :] = both.astype(BF16)

    def owned(index, m):
        n = index - m * g.idle
        return n, (n >= 0) & (n < g.owners)

    def rows_of(n):
        return pl.ds(pl.multiple_of(n * g.piece, 16), g.piece)

    def to_owner(m, d):
        peer, device = team_peer(d)
        n, valid = owned(peer, m)
        n = jnp.where(valid, n, 0)
        sems = (team_send, team_recv)
        at = team_in.at[m, d]
        return valid, remote(grad16.at[m, rows_of(n)], at, sems, m * g.team + d, device)

    def scatter(m):
        for d in range(1, g.team):
            valid, copy = to_owner(m, d)

            @pl.when(valid)
            def _():
                copy.start()

    def to_far(m, d):
        sems = (far_send, far_recv)
        here = far_in.at[m, z_hi]
        return remote(here, here, sems, m * g.far + d, far_peer(d))

    def add(m):
        n, mine = owned(me, m)

        @pl.when(mine)
        def _():
            total = grad16[m, rows_of(n), :].astype(F32)
            for d in range(1, g.team):
                to_owner(m, d)[1].wait_recv()
                total = total + team_in[m, d].astype(F32)
            far_in[m, z_hi] = total
            for d in range(1, g.far):
                to_far(m, d).start()

        for d in range(1, g.team):
            valid, copy = to_owner(m, d)

            @pl.when(valid)
            def _():
                copy.wait_send()

    def from_owner(m, d):
        n, _ = owned(me, m)
        there = gathered.at[m, core, rows_of(n)]
        sems = (back_send, back_recv)
        return remote(final.at[m], there, sems, m * g.team + d, team_peer(d)[1])

    def finish(m):
        n, mine = owned(me, m)

        @pl.when(mine)
        def _():
            for d in range(1, g.far):
                to_far(m, d).wait()
            total = far_in[m, 0]
            for f in range(1, g.far):
                total = total + far_in[m, f]
            final[m] = total.astype(BF16)
            for d in range(1, g.team):
                from_owner(m, d).start()
            gathered[m, core, rows_of(n), :] = final[m]

    swaps = [
        remote(
            gathered.at[m, core],
            gathered.at[m, core],
            (core_send, core_recv),
            g.chunks + m,
            sibling,
        )
        for m in range(g.chunks)
    ]

    def collect(m):
        n, mine = owned(me, m)
        for d in range(1, g.team):
            sender = lax.rem(me + g.team - d, g.team)
            valid = owned(sender, m)[1]
            sems = (back_send, back_recv)
            there = gathered.at[m, core, pl.ds(0, g.piece)]
            copy = remote(final.at[m], there, sems, m * g.team + d, team_peer(d)[1])

            @pl.when(valid)
            def _():
                copy.wait_recv()

        swaps[m].start()

        @pl.when(mine)
        def _():
            for d in range(1, g.team):
                from_owner(m, d).wait_send()

    def unfold(m):
        swaps[m].wait()
        for h in range(2):
            for k in range(g.k):
                at = k * g.c + m * g.wide + h * g.slim
                for b in range(g.blocks):
                    row = b * g.tier + k * g.slim
                    piece = gathered[m, h, row : row + g.slim, :].astype(F32) * g.scale
                    total_out[at : at + g.slim, b * 128 : (b + 1) * 128] = piece

    def inward(p, carry):
        total = jnp.dot(wt[...], sp[p], preferred_element_type=F32).astype(BF16)
        out_s[2 * p] = total[:, :128]
        out_s[2 * p + 1] = total[:, 128:]
        return carry

    spread(0)
    give(0)
    spread(1)
    give(1)
    keep(0)
    scatter(0)
    keep(1)
    scatter(1)
    lax.fori_loop(0, g.pairs, inward, 0)
    store_out = pltpu.make_async_copy(out_s, out, local_sem.at[3])
    store_out.start()
    add(0)
    add(1)
    finish(0)
    finish(1)
    collect(0)
    collect(1)
    unfold(0)
    unfold(1)
    store_out.wait()


def on_device(cotangent, layer_input, filter_values, weights, row_offset, reach):
    channels, rows, cols = cotangent.shape
    kernels, nlat, span, taps = filter_values.shape
    lat, lon = lax.axis_size("lat"), lax.axis_size("lon")
    g = Plan(lat, lon, channels, rows, cols, nlat, kernels, span, taps)
    anywhere = pl.BlockSpec(memory_space=pl.ANY)
    vmem = pl.BlockSpec(memory_space=pltpu.VMEM)
    dma = pltpu.SemaphoreType.DMA
    field = (rows, channels, cols)
    chunks = g.chunks
    out, total = pl.pallas_call(
        functools.partial(kernel, g),
        out_shape=(
            jax.ShapeDtypeStruct(field, BF16),
            jax.ShapeDtypeStruct((g.mix, channels), F32),
        ),
        in_specs=[anywhere, anywhere, anywhere, vmem, vmem, vmem],
        out_specs=(anywhere, vmem),
        scratch_shapes=[
            pltpu.VMEM((g.tall, channels, cols), BF16),
            pltpu.VMEM(field, BF16),
            pltpu.VMEM((rows * cols, channels), BF16),
            pltpu.VMEM((g.mix, channels), BF16),
            pltpu.VMEM((channels, g.mix), BF16),
            pltpu.VMEM((256, nlat), F32),
            pltpu.VMEM((kernels, g.near * 32, 128), F32),
            pltpu.VMEM((g.pairs, g.deep, kernels * 256), BF16),
            pltpu.VMEM((g.pairs, g.mix, 256), BF16),
            pltpu.VMEM((8 * rows, channels), BF16),
            pltpu.VMEM((8 * rows, channels), BF16),
            pltpu.VMEM((8 * rows + 64, channels), BF16),
            pltpu.VMEM((8 * rows + 64, channels), BF16),
            pltpu.VMEM((16 * g.tall, channels), BF16),
            pltpu.VMEM((g.pairs, channels, 128), BF16),
            pltpu.VMEM((chunks, g.half, 128), F32),
            pltpu.VMEM((chunks, g.half, 128), F32),
            pltpu.VMEM((chunks, g.half, 128), BF16),
            pltpu.VMEM((chunks, g.team, g.piece, 128), BF16),
            pltpu.VMEM((chunks, g.far, g.piece, 128), F32),
            pltpu.VMEM((chunks, g.piece, 128), BF16),
            pltpu.VMEM((chunks, 2, g.half, 128), BF16),
            pltpu.VMEM(field, BF16),
            dma((4,)),
            dma((8,)),
            dma((8,)),
            dma((2 * chunks,)),
            dma((2 * chunks,)),
            dma((chunks * g.team,)),
            dma((chunks * g.team,)),
            dma((chunks * g.far,)),
            dma((chunks * g.far,)),
            dma((chunks * g.team,)),
            dma((chunks * g.team,)),
        ],
        compiler_params=pltpu.CompilerParams(
            collective_id=0, has_side_effects=True, vmem_limit_bytes=56 * 2**20
        ),
    )(
        cotangent.transpose(1, 0, 2),
        layer_input.transpose(1, 0, 2),
        weights.reshape(kernels * channels, channels),
        filter_values.transpose(0, 3, 2, 1),
        row_offset,
        reach,
    )
    return out.transpose(1, 0, 2), total.reshape(kernels, channels, channels)


def solution(mesh):
    return jax.shard_map(
        on_device,
        mesh=mesh,
        in_specs=(P(None, "lat", "lon"), P(None, "lat", "lon"), P(), P(), P(), P()),
        out_specs=(P(None, "lat", "lon"), P()),
        check_vma=False,
    )
```

```python
import functools

import jax
import jax.numpy as jnp
from jax import lax
from jax.experimental import pallas as pl
from jax.experimental.pallas import tpu as pltpu
from jax.sharding import PartitionSpec as P

MESH = pl.DeviceIdType.MESH
F32 = jnp.float32
BF16 = jnp.bfloat16


def iota(shape, dim):
    return lax.broadcasted_iota(jnp.int32, shape, dim)


def ceil_to(n, m):
    return -(-n // m) * m


class Plan:
    def __init__(self, lat, lon, channels, rows, cols, nlat, kernels, span, taps):
        self.lat, self.lon = lat, lon
        self.c, self.rows, self.cols = channels, rows, cols
        self.nlat, self.k, self.span, self.taps = nlat, kernels, span, taps
        self.q = (taps - 1) // 2
        self.rim = span - 1
        self.tall = rows + 2 * self.rim
        self.near = 2 * span - 1
        self.pairs = rows // 2
        self.window = self.near + 1
        self.band = self.window * cols
        self.deep = self.band + self.window * 16
        self.mix = kernels * channels
        self.z = lat // 4
        self.far = self.z // 2
        self.team = 4 * lon
        self.chunks = 2
        self.wide = channels // self.chunks
        self.slim = self.wide // 2
        self.tier = kernels * self.slim
        self.blocks = channels // 128
        self.half = self.blocks * self.tier
        self.piece = ceil_to(-(-self.half // self.team), 16)
        self.owners = self.half // self.piece
        self.idle = self.team - self.owners


def remote(src, dst, sems, n, device):
    return pltpu.make_async_remote_copy(
        src_ref=src,
        dst_ref=dst,
        send_sem=sems[0].at[n],
        recv_sem=sems[1].at[n],
        device_id=device,
        device_id_type=MESH,
    )


def kernel(
    g,
    cot,
    xin,
    w_in,
    fv,
    ro,
    reach,
    out,
    total_out,
    cot_s,
    x_s,
    xt,
    w_s,
    wt,
    table,
    taps_s,
    toep,
    inner,
    sp,
    pack_l,
    pack_r,
    left,
    right,
    rim_s,
    rim_t,
    grad,
    core_in,
    grad16,
    team_in,
    far_in,
    final,
    out_s,
    local_sem,
    halo_send,
    halo_recv,
    core_send,
    core_recv,
    team_send,
    team_recv,
    far_send,
    far_recv,
    back_send,
    back_recv,
):
    lat = lax.axis_index("lat")
    lon = lax.axis_index("lon")
    core = lax.rem(lat, 2)
    zi = lax.rem(lat // 2, g.z)
    ylo = lat // (2 * g.z)
    z_lo, z_hi = lax.rem(zi, 2), zi // 2
    me = (ylo * g.lon + lon) * 2 + z_lo
    up, down = lax.rem(lat + 1, g.lat), lax.rem(lat + g.lat - 1, g.lat)
    east, west = lax.rem(lon + 1, g.lon), lax.rem(lon + g.lon - 1, g.lon)
    sibling = (lat + 1 - 2 * core, lon)

    def team_peer(d):
        peer = lax.rem(me + d, g.team)
        column = peer // 2
        z = 2 * z_hi + lax.rem(peer, 2)
        return peer, ((column // g.lon) * (2 * g.z) + 2 * z + core, lax.rem(column, g.lon))

    def far_peer(d):
        z = 2 * lax.rem(z_hi + d, g.far) + z_lo
        return (ylo * 2 * g.z + 2 * z + core, lon)

    halo = [
        (up, east),
        (up, west),
        (down, east),
        (down, west),
        (lat, east),
        (lat, west),
        (up, lon),
        (down, lon),
    ]
    partners = halo + [sibling]
    partners += [team_peer(d)[1] for d in range(1, g.team)]
    partners += [far_peer(d) for d in range(1, g.far)]

    barrier = pltpu.get_barrier_semaphore()
    for peer in partners:
        pl.semaphore_signal(barrier, inc=1, device_id=peer, device_id_type=MESH)

    load_cot = pltpu.make_async_copy(cot, cot_s.at[pl.ds(g.rim, g.rows)], local_sem.at[0])
    load_x = pltpu.make_async_copy(xin, x_s, local_sem.at[1])
    load_w = pltpu.make_async_copy(w_in, w_s, local_sem.at[2])
    load_cot.start()
    load_x.start()
    load_w.start()
    load_cot.wait()

    pick = iota((16, g.cols), 0)
    lane = iota((16, g.cols), 1)
    pick = (lane == jnp.where(pick < 8, pick + (g.cols - 8), pick - 8)).astype(F32).astype(BF16)
    for o in range(0, g.rows, 2):
        edge = [
            lax.dot_general(
                pick, cot_s[g.rim + o + n], (((1,), (1,)), ((), ())), preferred_element_type=F32
            )
            for n in range(2)
        ]
        pack_r[8 * o : 8 * o + 16, :] = jnp.concatenate([edge[0][:8], edge[1][:8]], 0).astype(BF16)
        pack_l[8 * o : 8 * o + 16, :] = jnp.concatenate([edge[0][8:], edge[1][8:]], 0).astype(BF16)

    pl.semaphore_wait(barrier, len(partners))

    sems = (halo_send, halo_recv)
    n_own = 8 * g.rows
    last = n_own - 32
    rim, tall, rows = g.rim, g.tall, g.rows
    sends = [
        remote(pack_r.at[pl.ds(last, 32)], left.at[pl.ds(0, 32)], sems, 0, halo[0]),
        remote(pack_l.at[pl.ds(last, 32)], right.at[pl.ds(0, 32)], sems, 1, halo[1]),
        remote(pack_r.at[pl.ds(0, 32)], left.at[pl.ds(32 + n_own, 32)], sems, 2, halo[2]),
        remote(pack_l.at[pl.ds(0, 32)], right.at[pl.ds(32 + n_own, 32)], sems, 3, halo[3]),
        remote(pack_r, left.at[pl.ds(32, n_own)], sems, 4, halo[4]),
        remote(pack_l, right.at[pl.ds(32, n_own)], sems, 5, halo[5]),
        remote(cot.at[pl.ds(rows - rim, rim)], cot_s.at[pl.ds(0, rim)], sems, 6, halo[6]),
        remote(cot.at[pl.ds(0, rim)], cot_s.at[pl.ds(tall - rim, rim)], sems, 7, halo[7]),
    ]
    for copy in sends:
        copy.start()

    entries = g.k * g.taps * g.span
    for k in range(g.k):
        for t in range(g.taps):
            n = (k * g.taps + t) * g.span
            table[n : n + g.span, :] = fv[k, t].astype(F32)
    table[entries:, :] = jnp.zeros((256 - entries, g.nlat), F32)
    source = iota((32, g.nlat), 1)
    slot = iota((32, g.nlat), 0)
    here = (source == lat * rows - rim + slot) & (slot < tall)
    moved = lax.dot_general(
        here.astype(F32).astype(BF16),
        table[...].astype(BF16),
        (((1,), (1,)), ((), ())),
        preferred_element_type=F32,
    )
    first = jnp.where(here, ro[...].astype(F32)[None, :], 0.0)
    first = jnp.sum(first, axis=1, keepdims=True).astype(jnp.int32)
    reached = jnp.where(here, reach[...].astype(F32)[None, :], 0.0)
    reached = jnp.sum(reached, axis=1, keepdims=True).astype(jnp.int32)
    column = iota((32, 256), 1)
    level = column & 3
    order = column >> 2
    tap = order
    for n in range(1, g.k):
        tap = tap - jnp.where(order >= n * g.taps, g.taps, 0)
    moved = jnp.where(jnp.abs(tap - g.q) < reached, moved, 0.0)
    levels = jnp.concatenate(
        [jnp.where(level == g.rim - j - first, moved, 0.0) for j in range(g.near)], 0
    ).astype(BF16)
    entry = iota((256, g.k * 128), 0) >> 2
    place = iota((256, g.k * 128), 1)
    offset = ((place & 127) + g.q) & 127
    wanted = (place >> 7) * g.taps + offset
    spot = ((entry == wanted) & (offset < g.taps)).astype(F32).astype(BF16)
    placed = jnp.dot(levels, spot, preferred_element_type=F32)
    for k in range(g.k):
        taps_s[k] = placed[:, k * 128 : (k + 1) * 128]

    l_in = iota((g.cols, g.cols), 0)
    l_out = iota((g.cols, g.cols), 1)
    near = jnp.abs(l_in - l_out) <= g.q
    m_in = iota((8, g.cols), 0)
    m_out = iota((8, g.cols), 1)
    from_left = m_out <= m_in
    from_right = m_out >= m_in + (g.cols - 8)

    def build(p, carry):
        early = p < g.pairs // 2
        band = jnp.where(early, g.window * 16, 0)
        ends = jnp.where(early, 0, g.band)

        def band_at(at):
            return pl.ds(pl.multiple_of(band + at * 128, 128), 128)

        def ends_at(at):
            return pl.ds(pl.multiple_of(ends + at * 16, 16), 16)

        for i in range(2):
            empty = (g.window - 1) * (1 - i)
            for k in range(g.k):
                lanes = slice((2 * k + i) * 128, (2 * k + i + 1) * 128)
                toep[p, band_at(empty), lanes] = jnp.zeros((128, 128), BF16)
                toep[p, ends_at(empty), lanes] = jnp.zeros((16, 128), BF16)
                for j in range(g.near):
                    row = taps_s[k, pl.ds(j * 32 + 2 * p + i + j, 1), :]
                    wheel = pltpu.roll(
                        jnp.broadcast_to(row, (128, 128)), 0, 1, stride=1, stride_axis=0
                    )
                    at = i + j
                    toep[p, band_at(at), lanes] = jnp.where(near, wheel, 0.0).astype(BF16)
                    corner = jnp.concatenate(
                        [
                            jnp.where(from_left, wheel[120:], 0.0),
                            jnp.where(from_right, wheel[:8], 0.0),
                        ],
                        0,
                    )
                    toep[p, ends_at(at), lanes] = corner.astype(BF16)
        return carry

    lax.fori_loop(0, g.pairs, build, 0)

    def own_rows(p):
        return max(0, rim - 2 * p), min(g.window, rim + rows - 2 * p)

    for p in range(g.pairs):
        low, high = own_rows(p)
        start = g.window * 16 if p < g.pairs // 2 else 0
        wide = jnp.concatenate([cot_s[2 * p + j] for j in range(low, high)], 1)
        deep = toep[p, start + low * 128 : start + high * 128, :]
        inner[p] = jnp.dot(wide, deep, preferred_element_type=F32)

    load_x.wait()
    load_w.wait()
    for i in range(rows):
        xt[i * 128 : (i + 1) * 128, :] = x_s[i].T
    for k in range(g.k):
        wt[:, k * g.c : (k + 1) * g.c] = w_s[k * g.c : (k + 1) * g.c, :].T

    def lay_rim(w):
        at = 16 * ((w + 1) // 2)
        odd = 8 * ((w + 1) % 2)
        rim_s[16 * w : 16 * w + 16, :] = jnp.concatenate(
            [
                left[at : at + 16, :].astype(F32)[odd : odd + 8],
                right[at : at + 16, :].astype(F32)[odd : odd + 8],
            ],
            0,
        ).astype(BF16)

    def spread(p, part):
        low, high = own_rows(p)
        ends = rim_t[p, part, :]
        if p < g.pairs // 2:
            wide = [ends] + [cot_s[2 * p + j, part, :] for j in range(low)]
            deep = toep[p, : g.window * 16 + low * 128, :]
        else:
            wide = [cot_s[2 * p + j, part, :] for j in range(high, g.window)] + [ends]
            deep = toep[p, high * 128 :, :]
        total = jnp.dot(jnp.concatenate(wide, 1), deep, preferred_element_type=F32)
        total = total + inner[p, part, :]
        for k in range(g.k):
            at = slice(k * g.c + part.start, k * g.c + part.stop)
            sp[p, at, :] = total[:, k * 256 : (k + 1) * 256].astype(BF16)

    def turn(p):
        rim_t[p] = rim_s[32 * p : 32 * p + 16 * g.window, :].T

    whole = [p for p in range(g.pairs) if own_rows(p) == (0, g.window)]
    others = [p for p in range(g.pairs) if p not in whole]
    for n in (4, 5):
        sends[n].wait()
    for w in range(rim + 1, tall - rim - 1):
        lay_rim(w)
    for p in whole:
        turn(p)
        spread(p, slice(0, g.c))
    for n in (0, 1, 2, 3, 6, 7):
        sends[n].wait()
    for w in list(range(rim + 1)) + list(range(tall - rim - 1, tall)):
        lay_rim(w)

    def chunk(m):
        for p in others:
            if m == 0:
                turn(p)
            spread(p, slice(m * g.wide, (m + 1) * g.wide))

    def term(m, h):
        tiers = []
        for k in range(g.k):
            at = pl.multiple_of(k * g.c + m * g.wide + h * g.slim, 32)
            tiers.append(
                jnp.concatenate([sp[p, pl.ds(at, g.slim), :] for p in range(g.pairs)], 1)
            )
        return jnp.dot(jnp.concatenate(tiers, 0), xt[...], preferred_element_type=F32)

    to_core = [
        remote(grad.at[m], core_in.at[m], (core_send, core_recv), m, sibling)
        for m in range(g.chunks)
    ]

    def give(m):
        total = term(m, 1 - core)
        for b in range(g.blocks):
            grad[m, b * g.tier : (b + 1) * g.tier, :] = total[:, b * 128 : (b + 1) * 128]
        to_core[m].start()

    def keep(m):
        total = term(m, core)
        to_core[m].wait()
        for b in range(g.blocks):
            at = slice(b * g.tier, (b + 1) * g.tier)
            both = total[:, b * 128 : (b + 1) * 128] + core_in[m, at, :]
            grad16[m, at, :] = both.astype(BF16)

    def owned(index, m):
        n = index - m * g.idle
        return n, (n >= 0) & (n < g.owners)

    def rows_of(n):
        return pl.ds(pl.multiple_of(n * g.piece, 16), g.piece)

    def to_owner(m, d):
        peer, device = team_peer(d)
        n, valid = owned(peer, m)
        n = jnp.where(valid, n, 0)
        sems = (team_send, team_recv)
        at = team_in.at[m, d]
        return valid, remote(grad16.at[m, rows_of(n)], at, sems, m * g.team + d, device)

    def scatter(m):
        for d in range(1, g.team):
            valid, copy = to_owner(m, d)

            @pl.when(valid)
            def _():
                copy.start()

    def to_far(m, d):
        sems = (far_send, far_recv)
        here = far_in.at[m, z_hi]
        return remote(here, here, sems, m * g.far + d, far_peer(d))

    def add(m):
        n, mine = owned(me, m)

        @pl.when(mine)
        def _():
            total = grad16[m, rows_of(n), :].astype(F32)
            for d in range(1, g.team):
                to_owner(m, d)[1].wait_recv()
                total = total + team_in[m, d].astype(F32)
            far_in[m, z_hi] = total
            for d in range(1, g.far):
                to_far(m, d).start()

        for d in range(1, g.team):
            valid, copy = to_owner(m, d)

            @pl.when(valid)
            def _():
                copy.wait_send()

    def landing(m, n):
        b, r = n // (g.tier // g.piece), lax.rem(n, g.tier // g.piece)
        k, r = r // (g.slim // g.piece), lax.rem(r, g.slim // g.piece)
        row = k * g.c + m * g.wide + core * g.slim + r * g.piece
        return total_out.at[
            pl.ds(pl.multiple_of(row, 32), g.piece), pl.ds(pl.multiple_of(b * 128, 128), 128)
        ]

    def from_owner(m, d):
        there = landing(m, owned(me, m)[0])
        sems = (back_send, back_recv)
        return remote(final.at[m], there, sems, m * g.team + d, team_peer(d)[1])

    def lay_own(m):
        there = landing(m, owned(me, m)[0])
        return pltpu.make_async_copy(final.at[m], there, local_sem.at[4 + m])

    def finish(m):
        n, mine = owned(me, m)

        @pl.when(mine)
        def _():
            for d in range(1, g.far):
                to_far(m, d).wait()
            total = far_in[m, 0]
            for f in range(1, g.far):
                total = total + far_in[m, f]
            final[m] = total.astype(BF16)
            for d in range(1, g.team):
                from_owner(m, d).start()
            lay_own(m).start()

    def swap(m, k):
        row = pl.multiple_of(k * g.c + m * g.wide + core * g.slim, 32)
        block = total_out.at[pl.ds(row, g.slim)]
        sems = (core_send, core_recv)
        return remote(block, block, sems, g.chunks + m * g.k + k, sibling)

    def collect(m):
        _, mine = owned(me, m)
        for d in range(1, g.team):
            sender = lax.rem(me + g.team - d, g.team)
            n, valid = owned(sender, m)
            n = jnp.where(valid, n, 0)
            sems = (back_send, back_recv)
            copy = remote(final.at[m], landing(m, n), sems, m * g.team + d, team_peer(d)[1])

            @pl.when(valid)
            def _():
                copy.wait_recv()

        @pl.when(mine)
        def _():
            lay_own(m).wait()

        for k in range(g.k):
            swap(m, k).start()

        @pl.when(mine)
        def _():
            for d in range(1, g.team):
                from_owner(m, d).wait_send()

    def inward(p, carry):
        total = jnp.dot(wt[...], sp[p], preferred_element_type=F32).astype(BF16)
        out_s[2 * p] = total[:, :128]
        out_s[2 * p + 1] = total[:, 128:]
        return carry

    chunk(0)
    give(0)
    chunk(1)
    give(1)
    keep(0)
    scatter(0)
    keep(1)
    scatter(1)
    lax.fori_loop(0, g.pairs, inward, 0)
    store_out = pltpu.make_async_copy(out_s, out, local_sem.at[3])
    store_out.start()
    add(0)
    add(1)
    finish(0)
    finish(1)
    collect(0)
    collect(1)
    for m in range(g.chunks):
        for k in range(g.k):
            swap(m, k).wait()
    store_out.wait()


def on_device(cotangent, layer_input, filter_values, weights, row_offset, reach):
    channels, rows, cols = cotangent.shape
    kernels, nlat, span, taps = filter_values.shape
    lat, lon = lax.axis_size("lat"), lax.axis_size("lon")
    g = Plan(lat, lon, channels, rows, cols, nlat, kernels, span, taps)
    anywhere = pl.BlockSpec(memory_space=pl.ANY)
    vmem = pl.BlockSpec(memory_space=pltpu.VMEM)
    dma = pltpu.SemaphoreType.DMA
    field = (rows, channels, cols)
    chunks = g.chunks
    out, total = pl.pallas_call(
        functools.partial(kernel, g),
        out_shape=(
            jax.ShapeDtypeStruct(field, BF16),
            jax.ShapeDtypeStruct((g.mix, channels), BF16),
        ),
        in_specs=[anywhere, anywhere, anywhere, vmem, vmem, vmem],
        out_specs=(anywhere, vmem),
        scratch_shapes=[
            pltpu.VMEM((g.tall, channels, cols), BF16),
            pltpu.VMEM(field, BF16),
            pltpu.VMEM((rows * cols, channels), BF16),
            pltpu.VMEM((g.mix, channels), BF16),
            pltpu.VMEM((channels, g.mix), BF16),
            pltpu.VMEM((256, nlat), F32),
            pltpu.VMEM((kernels, g.near * 32, 128), F32),
            pltpu.VMEM((g.pairs, g.deep, kernels * 256), BF16),
            pltpu.VMEM((g.pairs, channels, kernels * 256), F32),
            pltpu.VMEM((g.pairs, g.mix, 256), BF16),
            pltpu.VMEM((8 * rows, channels), BF16),
            pltpu.VMEM((8 * rows, channels), BF16),
            pltpu.VMEM((8 * rows + 64, channels), BF16),
            pltpu.VMEM((8 * rows + 64, channels), BF16),
            pltpu.VMEM((16 * g.tall, channels), BF16),
            pltpu.VMEM((g.pairs, channels, 128), BF16),
            pltpu.VMEM((chunks, g.half, 128), F32),
            pltpu.VMEM((chunks, g.half, 128), F32),
            pltpu.VMEM((chunks, g.half, 128), BF16),
            pltpu.VMEM((chunks, g.team, g.piece, 128), BF16),
            pltpu.VMEM((chunks, g.far, g.piece, 128), F32),
            pltpu.VMEM((chunks, g.piece, 128), BF16),
            pltpu.VMEM(field, BF16),
            dma((4 + chunks,)),
            dma((8,)),
            dma((8,)),
            dma((chunks * (1 + kernels),)),
            dma((chunks * (1 + kernels),)),
            dma((chunks * g.team,)),
            dma((chunks * g.team,)),
            dma((chunks * g.far,)),
            dma((chunks * g.far,)),
            dma((chunks * g.team,)),
            dma((chunks * g.team,)),
        ],
        compiler_params=pltpu.CompilerParams(
            collective_id=0, has_side_effects=True, vmem_limit_bytes=56 * 2**20
        ),
    )(
        cotangent.transpose(1, 0, 2),
        layer_input.transpose(1, 0, 2),
        weights.reshape(kernels * channels, channels),
        filter_values.transpose(0, 3, 2, 1),
        row_offset,
        reach,
    )
    weight_grad = total.reshape(kernels, channels, channels).astype(F32)
    return out.transpose(1, 0, 2), weight_grad / jnp.sqrt(jnp.float32(nlat * cols * lon))


def solution(mesh):
    return jax.shard_map(
        on_device,
        mesh=mesh,
        in_specs=(P(None, "lat", "lon"), P(None, "lat", "lon"), P(), P(), P(), P()),
        out_specs=(P(None, "lat", "lon"), P()),
        check_vma=False,
    )
```

```python
import functools

import jax
import jax.numpy as jnp
from jax import lax
from jax.experimental import pallas as pl
from jax.experimental.pallas import tpu as pltpu
from jax.sharding import PartitionSpec as P

MESH = pl.DeviceIdType.MESH
F32 = jnp.float32
BF16 = jnp.bfloat16


def iota(shape, dim):
    return lax.broadcasted_iota(jnp.int32, shape, dim)


def ceil_to(n, m):
    return -(-n // m) * m


class Plan:
    def __init__(self, lat, lon, channels, rows, cols, nlat, kernels, span, taps):
        self.lat, self.lon = lat, lon
        self.c, self.rows, self.cols = channels, rows, cols
        self.nlat, self.k, self.span, self.taps = nlat, kernels, span, taps
        self.q = (taps - 1) // 2
        self.rim = span - 1
        self.tall = rows + 2 * self.rim
        self.near = 2 * span - 1
        self.pairs = rows // 2
        self.window = self.near + 1
        self.band = self.window * cols
        self.deep = self.band + self.window * 16
        self.mix = kernels * channels
        self.z = lat // 4
        self.far = self.z // 2
        self.team = 4 * lon
        self.chunks = 2
        self.wide = channels // self.chunks
        self.slim = self.wide // 2
        self.tier = kernels * self.slim
        self.blocks = channels // 128
        self.half = self.blocks * self.tier
        self.piece = ceil_to(-(-self.half // self.team), 16)
        self.owners = self.half // self.piece
        self.idle = self.team - self.owners


def remote(src, dst, sems, n, device):
    return pltpu.make_async_remote_copy(
        src_ref=src,
        dst_ref=dst,
        send_sem=sems[0].at[n],
        recv_sem=sems[1].at[n],
        device_id=device,
        device_id_type=MESH,
    )


def kernel(
    g,
    cot,
    xin,
    w_in,
    fv,
    ro,
    reach,
    out,
    total_out,
    cot_s,
    x_s,
    xt,
    w_s,
    wt,
    table,
    taps_s,
    toep,
    inner,
    sp,
    pack_l,
    pack_r,
    left,
    right,
    rim_s,
    rim_t,
    grad,
    core_in,
    grad16,
    team_in,
    far_in,
    final,
    local_sem,
    halo_send,
    halo_recv,
    core_send,
    core_recv,
    team_send,
    team_recv,
    far_send,
    far_recv,
    back_send,
    back_recv,
):
    lat = lax.axis_index("lat")
    lon = lax.axis_index("lon")
    core = lax.rem(lat, 2)
    zi = lax.rem(lat // 2, g.z)
    ylo = lat // (2 * g.z)
    z_lo, z_hi = lax.rem(zi, 2), zi // 2
    me = (ylo * g.lon + lon) * 2 + z_lo
    up, down = lax.rem(lat + 1, g.lat), lax.rem(lat + g.lat - 1, g.lat)
    east, west = lax.rem(lon + 1, g.lon), lax.rem(lon + g.lon - 1, g.lon)
    sibling = (lat + 1 - 2 * core, lon)

    def team_peer(d):
        peer = lax.rem(me + d, g.team)
        column = peer // 2
        z = 2 * z_hi + lax.rem(peer, 2)
        return peer, ((column // g.lon) * (2 * g.z) + 2 * z + core, lax.rem(column, g.lon))

    def far_peer(d):
        z = 2 * lax.rem(z_hi + d, g.far) + z_lo
        return (ylo * 2 * g.z + 2 * z + core, lon)

    halo = [
        (up, east),
        (up, west),
        (down, east),
        (down, west),
        (lat, east),
        (lat, west),
        (up, lon),
        (down, lon),
    ]
    partners = halo + [sibling]
    partners += [team_peer(d)[1] for d in range(1, g.team)]
    partners += [far_peer(d) for d in range(1, g.far)]

    barrier = pltpu.get_barrier_semaphore()
    for peer in partners:
        pl.semaphore_signal(barrier, inc=1, device_id=peer, device_id_type=MESH)

    load_cot = pltpu.make_async_copy(cot, cot_s.at[pl.ds(g.rim, g.rows)], local_sem.at[0])
    load_x = pltpu.make_async_copy(xin, x_s, local_sem.at[1])
    load_w = pltpu.make_async_copy(w_in, w_s, local_sem.at[2])
    load_cot.start()
    load_x.start()
    load_w.start()
    load_cot.wait()

    pick = iota((16, g.cols), 0)
    lane = iota((16, g.cols), 1)
    pick = (lane == jnp.where(pick < 8, pick + (g.cols - 8), pick - 8)).astype(F32).astype(BF16)
    for o in range(0, g.rows, 2):
        edge = [
            lax.dot_general(
                pick, cot_s[g.rim + o + n], (((1,), (1,)), ((), ())), preferred_element_type=F32
            )
            for n in range(2)
        ]
        pack_r[8 * o : 8 * o + 16, :] = jnp.concatenate([edge[0][:8], edge[1][:8]], 0).astype(BF16)
        pack_l[8 * o : 8 * o + 16, :] = jnp.concatenate([edge[0][8:], edge[1][8:]], 0).astype(BF16)

    pl.semaphore_wait(barrier, len(partners))

    sems = (halo_send, halo_recv)
    n_own = 8 * g.rows
    last = n_own - 32
    rim, tall, rows = g.rim, g.tall, g.rows
    sends = [
        remote(pack_r.at[pl.ds(last, 32)], left.at[pl.ds(0, 32)], sems, 0, halo[0]),
        remote(pack_l.at[pl.ds(last, 32)], right.at[pl.ds(0, 32)], sems, 1, halo[1]),
        remote(pack_r.at[pl.ds(0, 32)], left.at[pl.ds(32 + n_own, 32)], sems, 2, halo[2]),
        remote(pack_l.at[pl.ds(0, 32)], right.at[pl.ds(32 + n_own, 32)], sems, 3, halo[3]),
        remote(pack_r, left.at[pl.ds(32, n_own)], sems, 4, halo[4]),
        remote(pack_l, right.at[pl.ds(32, n_own)], sems, 5, halo[5]),
        remote(cot.at[pl.ds(rows - rim, rim)], cot_s.at[pl.ds(0, rim)], sems, 6, halo[6]),
        remote(cot.at[pl.ds(0, rim)], cot_s.at[pl.ds(tall - rim, rim)], sems, 7, halo[7]),
    ]
    for copy in sends:
        copy.start()

    entries = g.k * g.taps * g.span
    for k in range(g.k):
        for t in range(g.taps):
            n = (k * g.taps + t) * g.span
            table[n : n + g.span, :] = fv[k, t].astype(F32)
    table[entries:, :] = jnp.zeros((256 - entries, g.nlat), F32)
    source = iota((32, g.nlat), 1)
    slot = iota((32, g.nlat), 0)
    here = (source == lat * rows - rim + slot) & (slot < tall)
    moved = lax.dot_general(
        here.astype(F32).astype(BF16),
        table[...].astype(BF16),
        (((1,), (1,)), ((), ())),
        preferred_element_type=F32,
    )
    first = jnp.where(here, ro[...].astype(F32)[None, :], 0.0)
    first = jnp.sum(first, axis=1, keepdims=True).astype(jnp.int32)
    reached = jnp.where(here, reach[...].astype(F32)[None, :], 0.0)
    reached = jnp.sum(reached, axis=1, keepdims=True).astype(jnp.int32)
    column = iota((32, 256), 1)
    level = column & 3
    order = column >> 2
    tap = order
    for n in range(1, g.k):
        tap = tap - jnp.where(order >= n * g.taps, g.taps, 0)
    moved = jnp.where(jnp.abs(tap - g.q) < reached, moved, 0.0)
    levels = jnp.concatenate(
        [jnp.where(level == g.rim - j - first, moved, 0.0) for j in range(g.near)], 0
    ).astype(BF16)
    entry = iota((256, g.k * 128), 0) >> 2
    place = iota((256, g.k * 128), 1)
    offset = ((place & 127) + g.q) & 127
    wanted = (place >> 7) * g.taps + offset
    spot = ((entry == wanted) & (offset < g.taps)).astype(F32).astype(BF16)
    placed = jnp.dot(levels, spot, preferred_element_type=F32)
    for k in range(g.k):
        taps_s[k] = placed[:, k * 128 : (k + 1) * 128]

    l_in = iota((g.cols, g.cols), 0)
    l_out = iota((g.cols, g.cols), 1)
    near = jnp.abs(l_in - l_out) <= g.q
    m_in = iota((8, g.cols), 0)
    m_out = iota((8, g.cols), 1)
    from_left = m_out <= m_in
    from_right = m_out >= m_in + (g.cols - 8)

    def build(p, carry):
        early = p < g.pairs // 2
        band = jnp.where(early, g.window * 16, 0)
        ends = jnp.where(early, 0, g.band)

        def band_at(at):
            return pl.ds(pl.multiple_of(band + at * 128, 128), 128)

        def ends_at(at):
            return pl.ds(pl.multiple_of(ends + at * 16, 16), 16)

        for i in range(2):
            empty = (g.window - 1) * (1 - i)
            for k in range(g.k):
                lanes = slice((2 * k + i) * 128, (2 * k + i + 1) * 128)
                toep[p, band_at(empty), lanes] = jnp.zeros((128, 128), BF16)
                toep[p, ends_at(empty), lanes] = jnp.zeros((16, 128), BF16)
                for j in range(g.near):
                    row = taps_s[k, pl.ds(j * 32 + 2 * p + i + j, 1), :]
                    wheel = pltpu.roll(
                        jnp.broadcast_to(row, (128, 128)), 0, 1, stride=1, stride_axis=0
                    )
                    at = i + j
                    toep[p, band_at(at), lanes] = jnp.where(near, wheel, 0.0).astype(BF16)
                    corner = jnp.concatenate(
                        [
                            jnp.where(from_left, wheel[120:], 0.0),
                            jnp.where(from_right, wheel[:8], 0.0),
                        ],
                        0,
                    )
                    toep[p, ends_at(at), lanes] = corner.astype(BF16)
        return carry

    lax.fori_loop(0, g.pairs, build, 0)

    def own_rows(p):
        return max(0, rim - 2 * p), min(g.window, rim + rows - 2 * p)

    for p in range(g.pairs):
        low, high = own_rows(p)
        start = g.window * 16 if p < g.pairs // 2 else 0
        wide = jnp.concatenate([cot_s[2 * p + j] for j in range(low, high)], 1)
        deep = toep[p, start + low * 128 : start + high * 128, :]
        inner[p] = jnp.dot(wide, deep, preferred_element_type=F32)

    load_x.wait()
    load_w.wait()
    for i in range(rows):
        xt[i * 128 : (i + 1) * 128, :] = x_s[i].T
    for k in range(g.k):
        wt[:, k * g.c : (k + 1) * g.c] = w_s[k * g.c : (k + 1) * g.c, :].T

    def lay_rim(w):
        at = 16 * ((w + 1) // 2)
        odd = 8 * ((w + 1) % 2)
        rim_s[16 * w : 16 * w + 16, :] = jnp.concatenate(
            [
                left[at : at + 16, :].astype(F32)[odd : odd + 8],
                right[at : at + 16, :].astype(F32)[odd : odd + 8],
            ],
            0,
        ).astype(BF16)

    def spread(p, part):
        low, high = own_rows(p)
        ends = rim_t[p, part, :]
        if p < g.pairs // 2:
            wide = [ends] + [cot_s[2 * p + j, part, :] for j in range(low)]
            deep = toep[p, : g.window * 16 + low * 128, :]
        else:
            wide = [cot_s[2 * p + j, part, :] for j in range(high, g.window)] + [ends]
            deep = toep[p, high * 128 :, :]
        total = jnp.dot(jnp.concatenate(wide, 1), deep, preferred_element_type=F32)
        total = total + inner[p, part, :]
        for k in range(g.k):
            at = slice(k * g.c + part.start, k * g.c + part.stop)
            sp[p, at, :] = total[:, k * 256 : (k + 1) * 256].astype(BF16)

    def turn(p):
        rim_t[p] = rim_s[32 * p : 32 * p + 16 * g.window, :].T

    whole = [p for p in range(g.pairs) if own_rows(p) == (0, g.window)]
    others = [p for p in range(g.pairs) if p not in whole]
    for n in (4, 5):
        sends[n].wait()
    for w in range(rim + 1, tall - rim - 1):
        lay_rim(w)
    for p in whole:
        turn(p)
        spread(p, slice(0, g.c))
    for n in (0, 1, 2, 3, 6, 7):
        sends[n].wait()
    for w in list(range(rim + 1)) + list(range(tall - rim - 1, tall)):
        lay_rim(w)

    def chunk(m):
        for p in others:
            if m == 0:
                turn(p)
            spread(p, slice(m * g.wide, (m + 1) * g.wide))

    def term(m, h):
        tiers = []
        for k in range(g.k):
            at = pl.multiple_of(k * g.c + m * g.wide + h * g.slim, 32)
            tiers.append(
                jnp.concatenate([sp[p, pl.ds(at, g.slim), :] for p in range(g.pairs)], 1)
            )
        return jnp.dot(jnp.concatenate(tiers, 0), xt[...], preferred_element_type=F32)

    to_core = [
        remote(grad.at[m], core_in.at[m], (core_send, core_recv), m, sibling)
        for m in range(g.chunks)
    ]

    def give(m):
        total = term(m, 1 - core)
        for b in range(g.blocks):
            grad[m, b * g.tier : (b + 1) * g.tier, :] = total[:, b * 128 : (b + 1) * 128]
        to_core[m].start()

    def keep(m):
        total = term(m, core)
        to_core[m].wait()
        for b in range(g.blocks):
            at = slice(b * g.tier, (b + 1) * g.tier)
            both = total[:, b * 128 : (b + 1) * 128] + core_in[m, at, :]
            grad16[m, at, :] = both.astype(BF16)

    def owned(index, m):
        n = index - m * g.idle
        return n, (n >= 0) & (n < g.owners)

    def rows_of(n):
        return pl.ds(pl.multiple_of(n * g.piece, 16), g.piece)

    def to_owner(m, d):
        peer, device = team_peer(d)
        n, valid = owned(peer, m)
        n = jnp.where(valid, n, 0)
        sems = (team_send, team_recv)
        at = team_in.at[m, d]
        return valid, remote(grad16.at[m, rows_of(n)], at, sems, m * g.team + d, device)

    def scatter(m):
        for d in range(1, g.team):
            valid, copy = to_owner(m, d)

            @pl.when(valid)
            def _():
                copy.start()

    def to_far(m, d):
        sems = (far_send, far_recv)
        here = far_in.at[m, z_hi]
        return remote(here, here, sems, m * g.far + d, far_peer(d))

    def add(m):
        n, mine = owned(me, m)

        @pl.when(mine)
        def _():
            total = grad16[m, rows_of(n), :].astype(F32)
            for d in range(1, g.team):
                to_owner(m, d)[1].wait_recv()
                total = total + team_in[m, d].astype(F32)
            far_in[m, z_hi] = total
            for d in range(1, g.far):
                to_far(m, d).start()

        for d in range(1, g.team):
            valid, copy = to_owner(m, d)

            @pl.when(valid)
            def _():
                copy.wait_send()

    def landing(m, n):
        b, r = n // (g.tier // g.piece), lax.rem(n, g.tier // g.piece)
        k, r = r // (g.slim // g.piece), lax.rem(r, g.slim // g.piece)
        row = k * g.c + m * g.wide + core * g.slim + r * g.piece
        return total_out.at[
            pl.ds(pl.multiple_of(row, 32), g.piece), pl.ds(pl.multiple_of(b * 128, 128), 128)
        ]

    def from_owner(m, d):
        there = landing(m, owned(me, m)[0])
        sems = (back_send, back_recv)
        return remote(final.at[m], there, sems, m * g.team + d, team_peer(d)[1])

    def lay_own(m):
        there = landing(m, owned(me, m)[0])
        return pltpu.make_async_copy(final.at[m], there, local_sem.at[3 + m])

    def finish(m):
        n, mine = owned(me, m)

        @pl.when(mine)
        def _():
            for d in range(1, g.far):
                to_far(m, d).wait()
            total = far_in[m, 0]
            for f in range(1, g.far):
                total = total + far_in[m, f]
            final[m] = total.astype(BF16)
            for d in range(1, g.team):
                from_owner(m, d).start()
            lay_own(m).start()

    def swap(m, k):
        row = pl.multiple_of(k * g.c + m * g.wide + core * g.slim, 32)
        block = total_out.at[pl.ds(row, g.slim)]
        sems = (core_send, core_recv)
        return remote(block, block, sems, g.chunks + m * g.k + k, sibling)

    def collect(m):
        _, mine = owned(me, m)
        for d in range(1, g.team):
            sender = lax.rem(me + g.team - d, g.team)
            n, valid = owned(sender, m)
            n = jnp.where(valid, n, 0)
            sems = (back_send, back_recv)
            copy = remote(final.at[m], landing(m, n), sems, m * g.team + d, team_peer(d)[1])

            @pl.when(valid)
            def _():
                copy.wait_recv()

        @pl.when(mine)
        def _():
            lay_own(m).wait()

        for k in range(g.k):
            swap(m, k).start()

        @pl.when(mine)
        def _():
            for d in range(1, g.team):
                from_owner(m, d).wait_send()

    def inward(p, carry):
        total = jnp.dot(wt[...], sp[p], preferred_element_type=F32).astype(BF16)
        out[2 * p] = total[:, :128]
        out[2 * p + 1] = total[:, 128:]
        return carry

    chunk(0)
    give(0)
    chunk(1)
    give(1)
    keep(0)
    scatter(0)
    keep(1)
    scatter(1)
    lax.fori_loop(0, g.pairs, inward, 0)
    add(0)
    add(1)
    finish(0)
    finish(1)
    collect(0)
    collect(1)
    for m in range(g.chunks):
        for k in range(g.k):
            swap(m, k).wait()


def on_device(cotangent, layer_input, filter_values, weights, row_offset, reach):
    channels, rows, cols = cotangent.shape
    kernels, nlat, span, taps = filter_values.shape
    lat, lon = lax.axis_size("lat"), lax.axis_size("lon")
    g = Plan(lat, lon, channels, rows, cols, nlat, kernels, span, taps)
    anywhere = pl.BlockSpec(memory_space=pl.ANY)
    vmem = pl.BlockSpec(memory_space=pltpu.VMEM)
    dma = pltpu.SemaphoreType.DMA
    field = (rows, channels, cols)
    chunks = g.chunks
    out, total = pl.pallas_call(
        functools.partial(kernel, g),
        out_shape=(
            pltpu.VMEM(field, BF16),
            pltpu.VMEM((g.mix, channels), BF16),
        ),
        in_specs=[anywhere, anywhere, anywhere, vmem, vmem, vmem],
        out_specs=(vmem, vmem),
        scratch_shapes=[
            pltpu.VMEM((g.tall, channels, cols), BF16),
            pltpu.VMEM(field, BF16),
            pltpu.VMEM((rows * cols, channels), BF16),
            pltpu.VMEM((g.mix, channels), BF16),
            pltpu.VMEM((channels, g.mix), BF16),
            pltpu.VMEM((256, nlat), F32),
            pltpu.VMEM((kernels, g.near * 32, 128), F32),
            pltpu.VMEM((g.pairs, g.deep, kernels * 256), BF16),
            pltpu.VMEM((g.pairs, channels, kernels * 256), F32),
            pltpu.VMEM((g.pairs, g.mix, 256), BF16),
            pltpu.VMEM((8 * rows, channels), BF16),
            pltpu.VMEM((8 * rows, channels), BF16),
            pltpu.VMEM((8 * rows + 64, channels), BF16),
            pltpu.VMEM((8 * rows + 64, channels), BF16),
            pltpu.VMEM((16 * g.tall, channels), BF16),
            pltpu.VMEM((g.pairs, channels, 128), BF16),
            pltpu.VMEM((chunks, g.half, 128), F32),
            pltpu.VMEM((chunks, g.half, 128), F32),
            pltpu.VMEM((chunks, g.half, 128), BF16),
            pltpu.VMEM((chunks, g.team, g.piece, 128), BF16),
            pltpu.VMEM((chunks, g.far, g.piece, 128), F32),
            pltpu.VMEM((chunks, g.piece, 128), BF16),
            dma((3 + chunks,)),
            dma((8,)),
            dma((8,)),
            dma((chunks * (1 + kernels),)),
            dma((chunks * (1 + kernels),)),
            dma((chunks * g.team,)),
            dma((chunks * g.team,)),
            dma((chunks * g.far,)),
            dma((chunks * g.far,)),
            dma((chunks * g.team,)),
            dma((chunks * g.team,)),
        ],
        compiler_params=pltpu.CompilerParams(
            collective_id=0, has_side_effects=True, vmem_limit_bytes=56 * 2**20
        ),
    )(
        cotangent.transpose(1, 0, 2),
        layer_input.transpose(1, 0, 2),
        weights.reshape(kernels * channels, channels),
        filter_values.transpose(0, 3, 2, 1),
        row_offset,
        reach,
    )
    weight_grad = total.reshape(kernels, channels, channels).astype(F32)
    return out.transpose(1, 0, 2), weight_grad / jnp.sqrt(jnp.float32(nlat * cols * lon))


def solution(mesh):
    return jax.shard_map(
        on_device,
        mesh=mesh,
        in_specs=(P(None, "lat", "lon"), P(None, "lat", "lon"), P(), P(), P(), P()),
        out_specs=(P(None, "lat", "lon"), P()),
        check_vma=False,
    )
```

```python
import functools
import math

import jax
import jax.numpy as jnp
from jax import lax
from jax.experimental import pallas as pl
from jax.experimental.pallas import tpu as pltpu
from jax.sharding import PartitionSpec as P

MESH = pl.DeviceIdType.MESH
F32 = jnp.float32
BF16 = jnp.bfloat16


def iota(shape, dim):
    return lax.broadcasted_iota(jnp.int32, shape, dim)


def ceil_to(n, m):
    return -(-n // m) * m


class Plan:
    def __init__(self, lat, lon, channels, rows, cols, nlat, kernels, span, taps):
        self.lat, self.lon = lat, lon
        self.c, self.rows, self.cols = channels, rows, cols
        self.nlat, self.k, self.span, self.taps = nlat, kernels, span, taps
        self.q = (taps - 1) // 2
        self.rim = span - 1
        self.tall = rows + 2 * self.rim
        self.near = 2 * span - 1
        self.pairs = rows // 2
        self.window = self.near + 1
        self.band = self.window * cols
        self.deep = self.band + self.window * 16
        self.mix = kernels * channels
        self.z = lat // 4
        self.far = self.z // 2
        self.team = 4 * lon
        self.chunks = 2
        self.wide = channels // self.chunks
        self.slim = self.wide // 2
        self.tier = kernels * self.slim
        self.blocks = channels // 128
        self.half = self.blocks * self.tier
        self.piece = ceil_to(-(-self.half // self.team), 16)
        self.owners = self.half // self.piece
        self.idle = self.team - self.owners


def remote(src, dst, sems, n, device):
    return pltpu.make_async_remote_copy(
        src_ref=src,
        dst_ref=dst,
        send_sem=sems[0].at[n],
        recv_sem=sems[1].at[n],
        device_id=device,
        device_id_type=MESH,
    )


def kernel(
    g,
    cot,
    xin,
    w_in,
    fv_in,
    ro_in,
    reach_in,
    out,
    total_out,
    fv,
    ro,
    reach,
    cot_s,
    x_s,
    xt,
    w_s,
    wt,
    table,
    taps_s,
    toep,
    inner,
    sp,
    pack_l,
    pack_r,
    left,
    right,
    rim_s,
    rim_t,
    grad,
    core_in,
    grad16,
    team_in,
    far_in,
    final,
    local_sem,
    halo_send,
    halo_recv,
    core_send,
    core_recv,
    team_send,
    team_recv,
    far_send,
    far_recv,
    back_send,
    back_recv,
):
    lat = lax.axis_index("lat")
    lon = lax.axis_index("lon")
    core = lax.rem(lat, 2)
    zi = lax.rem(lat // 2, g.z)
    ylo = lat // (2 * g.z)
    z_lo, z_hi = lax.rem(zi, 2), zi // 2
    me = (ylo * g.lon + lon) * 2 + z_lo
    up, down = lax.rem(lat + 1, g.lat), lax.rem(lat + g.lat - 1, g.lat)
    east, west = lax.rem(lon + 1, g.lon), lax.rem(lon + g.lon - 1, g.lon)
    sibling = (lat + 1 - 2 * core, lon)

    def team_peer(d):
        peer = lax.rem(me + d, g.team)
        column = peer // 2
        z = 2 * z_hi + lax.rem(peer, 2)
        return peer, ((column // g.lon) * (2 * g.z) + 2 * z + core, lax.rem(column, g.lon))

    def far_peer(d):
        z = 2 * lax.rem(z_hi + d, g.far) + z_lo
        return (ylo * 2 * g.z + 2 * z + core, lon)

    halo = [
        (up, east),
        (up, west),
        (down, east),
        (down, west),
        (lat, east),
        (lat, west),
        (up, lon),
        (down, lon),
    ]
    partners = halo + [sibling]
    partners += [team_peer(d)[1] for d in range(1, g.team)]
    partners += [far_peer(d) for d in range(1, g.far)]

    barrier = pltpu.get_barrier_semaphore()
    for peer in partners:
        pl.semaphore_signal(barrier, inc=1, device_id=peer, device_id_type=MESH)

    load_cot = pltpu.make_async_copy(cot, cot_s.at[pl.ds(g.rim, g.rows)], local_sem.at[0])
    load_x = pltpu.make_async_copy(xin, x_s, local_sem.at[1])
    load_w = pltpu.make_async_copy(w_in, w_s, local_sem.at[2])
    load_taps = [
        pltpu.make_async_copy(source, target, local_sem.at[3 + g.chunks + n])
        for n, (source, target) in enumerate(((fv_in, fv), (ro_in, ro), (reach_in, reach)))
    ]
    load_cot.start()
    for copy in load_taps:
        copy.start()
    load_x.start()
    load_w.start()
    load_cot.wait()

    pick = iota((16, g.cols), 0)
    lane = iota((16, g.cols), 1)
    pick = (lane == jnp.where(pick < 8, pick + (g.cols - 8), pick - 8)).astype(F32).astype(BF16)
    for o in range(0, g.rows, 2):
        edge = [
            lax.dot_general(
                pick, cot_s[g.rim + o + n], (((1,), (1,)), ((), ())), preferred_element_type=F32
            )
            for n in range(2)
        ]
        pack_r[8 * o : 8 * o + 16, :] = jnp.concatenate([edge[0][:8], edge[1][:8]], 0).astype(BF16)
        pack_l[8 * o : 8 * o + 16, :] = jnp.concatenate([edge[0][8:], edge[1][8:]], 0).astype(BF16)

    pl.semaphore_wait(barrier, len(partners))

    sems = (halo_send, halo_recv)
    n_own = 8 * g.rows
    last = n_own - 32
    rim, tall, rows = g.rim, g.tall, g.rows
    sends = [
        remote(pack_r.at[pl.ds(last, 32)], left.at[pl.ds(0, 32)], sems, 0, halo[0]),
        remote(pack_l.at[pl.ds(last, 32)], right.at[pl.ds(0, 32)], sems, 1, halo[1]),
        remote(pack_r.at[pl.ds(0, 32)], left.at[pl.ds(32 + n_own, 32)], sems, 2, halo[2]),
        remote(pack_l.at[pl.ds(0, 32)], right.at[pl.ds(32 + n_own, 32)], sems, 3, halo[3]),
        remote(pack_r, left.at[pl.ds(32, n_own)], sems, 4, halo[4]),
        remote(pack_l, right.at[pl.ds(32, n_own)], sems, 5, halo[5]),
        remote(cot.at[pl.ds(rows - rim, rim)], cot_s.at[pl.ds(0, rim)], sems, 6, halo[6]),
        remote(cot.at[pl.ds(0, rim)], cot_s.at[pl.ds(tall - rim, rim)], sems, 7, halo[7]),
    ]
    for copy in sends:
        copy.start()

    for copy in load_taps:
        copy.wait()
    entries = g.k * g.taps * g.span
    for k in range(g.k):
        for t in range(g.taps):
            n = (k * g.taps + t) * g.span
            table[n : n + g.span, :] = fv[k, t].astype(F32)
    table[entries:, :] = jnp.zeros((256 - entries, g.nlat), F32)
    source = iota((32, g.nlat), 1)
    slot = iota((32, g.nlat), 0)
    here = (source == lat * rows - rim + slot) & (slot < tall)
    moved = lax.dot_general(
        here.astype(F32).astype(BF16),
        table[...].astype(BF16),
        (((1,), (1,)), ((), ())),
        preferred_element_type=F32,
    )
    first = jnp.where(here, ro[...].astype(F32)[None, :], 0.0)
    first = jnp.sum(first, axis=1, keepdims=True).astype(jnp.int32)
    reached = jnp.where(here, reach[...].astype(F32)[None, :], 0.0)
    reached = jnp.sum(reached, axis=1, keepdims=True).astype(jnp.int32)
    column = iota((32, 256), 1)
    level = column & 3
    order = column >> 2
    tap = order
    for n in range(1, g.k):
        tap = tap - jnp.where(order >= n * g.taps, g.taps, 0)
    moved = jnp.where(jnp.abs(tap - g.q) < reached, moved, 0.0)
    levels = jnp.concatenate(
        [jnp.where(level == g.rim - j - first, moved, 0.0) for j in range(g.near)], 0
    ).astype(BF16)
    entry = iota((256, g.k * 128), 0) >> 2
    place = iota((256, g.k * 128), 1)
    offset = ((place & 127) + g.q) & 127
    wanted = (place >> 7) * g.taps + offset
    spot = ((entry == wanted) & (offset < g.taps)).astype(F32).astype(BF16)
    placed = jnp.dot(levels, spot, preferred_element_type=F32)
    for k in range(g.k):
        taps_s[k] = placed[:, k * 128 : (k + 1) * 128]

    l_in = iota((g.cols, g.cols), 0)
    l_out = iota((g.cols, g.cols), 1)
    near = jnp.abs(l_in - l_out) <= g.q
    m_in = iota((8, g.cols), 0)
    m_out = iota((8, g.cols), 1)
    from_left = m_out <= m_in
    from_right = m_out >= m_in + (g.cols - 8)

    def build(p, carry):
        early = p < g.pairs // 2
        band = jnp.where(early, g.window * 16, 0)
        ends = jnp.where(early, 0, g.band)

        def band_at(at):
            return pl.ds(pl.multiple_of(band + at * 128, 128), 128)

        def ends_at(at):
            return pl.ds(pl.multiple_of(ends + at * 16, 16), 16)

        for i in range(2):
            empty = (g.window - 1) * (1 - i)
            for k in range(g.k):
                lanes = slice((2 * k + i) * 128, (2 * k + i + 1) * 128)
                toep[p, band_at(empty), lanes] = jnp.zeros((128, 128), BF16)
                toep[p, ends_at(empty), lanes] = jnp.zeros((16, 128), BF16)
                for j in range(g.near):
                    row = taps_s[k, pl.ds(j * 32 + 2 * p + i + j, 1), :]
                    wheel = pltpu.roll(
                        jnp.broadcast_to(row, (128, 128)), 0, 1, stride=1, stride_axis=0
                    )
                    at = i + j
                    toep[p, band_at(at), lanes] = jnp.where(near, wheel, 0.0).astype(BF16)
                    corner = jnp.concatenate(
                        [
                            jnp.where(from_left, wheel[120:], 0.0),
                            jnp.where(from_right, wheel[:8], 0.0),
                        ],
                        0,
                    )
                    toep[p, ends_at(at), lanes] = corner.astype(BF16)
        return carry

    lax.fori_loop(0, g.pairs, build, 0)

    def own_rows(p):
        return max(0, rim - 2 * p), min(g.window, rim + rows - 2 * p)

    for p in range(g.pairs):
        low, high = own_rows(p)
        start = g.window * 16 if p < g.pairs // 2 else 0
        wide = jnp.concatenate([cot_s[2 * p + j] for j in range(low, high)], 1)
        deep = toep[p, start + low * 128 : start + high * 128, :]
        inner[p] = jnp.dot(wide, deep, preferred_element_type=F32)

    load_x.wait()
    load_w.wait()
    for i in range(rows):
        xt[i * 128 : (i + 1) * 128, :] = x_s[i].T
    for k in range(g.k):
        wt[:, k * g.c : (k + 1) * g.c] = w_s[k * g.c : (k + 1) * g.c, :].T

    def lay_rim(w):
        at = 16 * ((w + 1) // 2)
        odd = 8 * ((w + 1) % 2)
        rim_s[16 * w : 16 * w + 16, :] = jnp.concatenate(
            [
                left[at : at + 16, :].astype(F32)[odd : odd + 8],
                right[at : at + 16, :].astype(F32)[odd : odd + 8],
            ],
            0,
        ).astype(BF16)

    def spread(p, part):
        low, high = own_rows(p)
        ends = rim_t[p, part, :]
        if p < g.pairs // 2:
            wide = [ends] + [cot_s[2 * p + j, part, :] for j in range(low)]
            deep = toep[p, : g.window * 16 + low * 128, :]
        else:
            wide = [cot_s[2 * p + j, part, :] for j in range(high, g.window)] + [ends]
            deep = toep[p, high * 128 :, :]
        total = jnp.dot(jnp.concatenate(wide, 1), deep, preferred_element_type=F32)
        total = total + inner[p, part, :]
        for k in range(g.k):
            at = slice(k * g.c + part.start, k * g.c + part.stop)
            sp[p, at, :] = total[:, k * 256 : (k + 1) * 256].astype(BF16)

    def turn(p):
        rim_t[p] = rim_s[32 * p : 32 * p + 16 * g.window, :].T

    whole = [p for p in range(g.pairs) if own_rows(p) == (0, g.window)]
    others = [p for p in range(g.pairs) if p not in whole]
    for n in (4, 5):
        sends[n].wait()
    for w in range(rim + 1, tall - rim - 1):
        lay_rim(w)
    for p in whole:
        turn(p)
        spread(p, slice(0, g.c))
    for n in (0, 1, 2, 3, 6, 7):
        sends[n].wait()
    for w in list(range(rim + 1)) + list(range(tall - rim - 1, tall)):
        lay_rim(w)

    def chunk(m):
        for p in others:
            if m == 0:
                turn(p)
            spread(p, slice(m * g.wide, (m + 1) * g.wide))

    def term(m, h):
        tiers = []
        for k in range(g.k):
            at = pl.multiple_of(k * g.c + m * g.wide + h * g.slim, 32)
            tiers.append(
                jnp.concatenate([sp[p, pl.ds(at, g.slim), :] for p in range(g.pairs)], 1)
            )
        return jnp.dot(jnp.concatenate(tiers, 0), xt[...], preferred_element_type=F32)

    to_core = [
        remote(grad.at[m], core_in.at[m], (core_send, core_recv), m, sibling)
        for m in range(g.chunks)
    ]

    def give(m):
        total = term(m, 1 - core)
        for b in range(g.blocks):
            grad[m, b * g.tier : (b + 1) * g.tier, :] = total[:, b * 128 : (b + 1) * 128]
        to_core[m].start()

    def keep(m):
        total = term(m, core)
        to_core[m].wait()
        for b in range(g.blocks):
            at = slice(b * g.tier, (b + 1) * g.tier)
            both = total[:, b * 128 : (b + 1) * 128] + core_in[m, at, :]
            grad16[m, at, :] = both.astype(BF16)

    def owned(index, m):
        n = index - m * g.idle
        return n, (n >= 0) & (n < g.owners)

    def rows_of(n):
        return pl.ds(pl.multiple_of(n * g.piece, 16), g.piece)

    def to_owner(m, d):
        peer, device = team_peer(d)
        n, valid = owned(peer, m)
        n = jnp.where(valid, n, 0)
        sems = (team_send, team_recv)
        at = team_in.at[m, d]
        return valid, remote(grad16.at[m, rows_of(n)], at, sems, m * g.team + d, device)

    def scatter(m):
        for d in range(1, g.team):
            valid, copy = to_owner(m, d)

            @pl.when(valid)
            def _():
                copy.start()

    def to_far(m, d):
        sems = (far_send, far_recv)
        here = far_in.at[m, z_hi]
        return remote(here, here, sems, m * g.far + d, far_peer(d))

    def add(m):
        n, mine = owned(me, m)

        @pl.when(mine)
        def _():
            total = grad16[m, rows_of(n), :].astype(F32)
            for d in range(1, g.team):
                to_owner(m, d)[1].wait_recv()
                total = total + team_in[m, d].astype(F32)
            far_in[m, z_hi] = total
            for d in range(1, g.far):
                to_far(m, d).start()

        for d in range(1, g.team):
            valid, copy = to_owner(m, d)

            @pl.when(valid)
            def _():
                copy.wait_send()

    def landing(m, n):
        b, r = n // (g.tier // g.piece), lax.rem(n, g.tier // g.piece)
        k, r = r // (g.slim // g.piece), lax.rem(r, g.slim // g.piece)
        row = k * g.c + m * g.wide + core * g.slim + r * g.piece
        return total_out.at[
            pl.ds(pl.multiple_of(row, 32), g.piece), pl.ds(pl.multiple_of(b * 128, 128), 128)
        ]

    def from_owner(m, d):
        there = landing(m, owned(me, m)[0])
        sems = (back_send, back_recv)
        return remote(final.at[m], there, sems, m * g.team + d, team_peer(d)[1])

    def lay_own(m):
        there = landing(m, owned(me, m)[0])
        return pltpu.make_async_copy(final.at[m], there, local_sem.at[3 + m])

    def finish(m):
        n, mine = owned(me, m)

        @pl.when(mine)
        def _():
            for d in range(1, g.far):
                to_far(m, d).wait()
            total = far_in[m, 0]
            for f in range(1, g.far):
                total = total + far_in[m, f]
            final[m] = total.astype(BF16)
            for d in range(1, g.team):
                from_owner(m, d).start()
            lay_own(m).start()

    def swap(m, k):
        row = pl.multiple_of(k * g.c + m * g.wide + core * g.slim, 32)
        block = total_out.at[pl.ds(row, g.slim)]
        sems = (core_send, core_recv)
        return remote(block, block, sems, g.chunks + m * g.k + k, sibling)

    def collect(m):
        _, mine = owned(me, m)
        for d in range(1, g.team):
            sender = lax.rem(me + g.team - d, g.team)
            n, valid = owned(sender, m)
            n = jnp.where(valid, n, 0)
            sems = (back_send, back_recv)
            copy = remote(final.at[m], landing(m, n), sems, m * g.team + d, team_peer(d)[1])

            @pl.when(valid)
            def _():
                copy.wait_recv()

        @pl.when(mine)
        def _():
            lay_own(m).wait()

        for k in range(g.k):
            swap(m, k).start()

        @pl.when(mine)
        def _():
            for d in range(1, g.team):
                from_owner(m, d).wait_send()

    def inward(p, carry):
        total = jnp.dot(wt[...], sp[p], preferred_element_type=F32).astype(BF16)
        out[2 * p] = total[:, :128]
        out[2 * p + 1] = total[:, 128:]
        return carry

    chunk(0)
    give(0)
    chunk(1)
    give(1)
    keep(0)
    scatter(0)
    keep(1)
    scatter(1)
    lax.fori_loop(0, g.pairs, inward, 0)
    add(0)
    add(1)
    finish(0)
    finish(1)
    collect(0)
    collect(1)
    for m in range(g.chunks):
        for k in range(g.k):
            swap(m, k).wait()


def deliver(scale, field, total, out, weight_grad, wide, sems):
    store = [pltpu.make_async_copy(field, out, sems.at[0])]
    store[0].start()
    kernels, channels, _ = wide.shape
    for k in range(kernels):
        wide[k] = total[k * channels : (k + 1) * channels, :].astype(F32) * scale
        store.append(pltpu.make_async_copy(wide.at[k], weight_grad.at[k], sems.at[1 + k]))
        store[-1].start()
    for copy in store:
        copy.wait()


def on_device(cotangent, layer_input, filter_values, weights, row_offset, reach):
    channels, rows, cols = cotangent.shape
    kernels, nlat, span, taps = filter_values.shape
    lat, lon = lax.axis_size("lat"), lax.axis_size("lon")
    g = Plan(lat, lon, channels, rows, cols, nlat, kernels, span, taps)
    anywhere = pl.BlockSpec(memory_space=pl.ANY)
    vmem = pl.BlockSpec(memory_space=pltpu.VMEM)
    dma = pltpu.SemaphoreType.DMA
    field = (rows, channels, cols)
    chunks = g.chunks
    out, total = pl.pallas_call(
        functools.partial(kernel, g),
        out_shape=(
            pltpu.VMEM(field, BF16),
            pltpu.VMEM((g.mix, channels), BF16),
        ),
        in_specs=[anywhere] * 6,
        out_specs=(vmem, vmem),
        scratch_shapes=[
            pltpu.VMEM((kernels, taps, span, nlat), BF16),
            pltpu.VMEM((nlat,), jnp.int32),
            pltpu.VMEM((nlat,), jnp.int32),
            pltpu.VMEM((g.tall, channels, cols), BF16),
            pltpu.VMEM(field, BF16),
            pltpu.VMEM((rows * cols, channels), BF16),
            pltpu.VMEM((g.mix, channels), BF16),
            pltpu.VMEM((channels, g.mix), BF16),
            pltpu.VMEM((256, nlat), F32),
            pltpu.VMEM((kernels, g.near * 32, 128), F32),
            pltpu.VMEM((g.pairs, g.deep, kernels * 256), BF16),
            pltpu.VMEM((g.pairs, channels, kernels * 256), F32),
            pltpu.VMEM((g.pairs, g.mix, 256), BF16),
            pltpu.VMEM((8 * rows, channels), BF16),
            pltpu.VMEM((8 * rows, channels), BF16),
            pltpu.VMEM((8 * rows + 64, channels), BF16),
            pltpu.VMEM((8 * rows + 64, channels), BF16),
            pltpu.VMEM((16 * g.tall, channels), BF16),
            pltpu.VMEM((g.pairs, channels, 128), BF16),
            pltpu.VMEM((chunks, g.half, 128), F32),
            pltpu.VMEM((chunks, g.half, 128), F32),
            pltpu.VMEM((chunks, g.half, 128), BF16),
            pltpu.VMEM((chunks, g.team, g.piece, 128), BF16),
            pltpu.VMEM((chunks, g.far, g.piece, 128), F32),
            pltpu.VMEM((chunks, g.piece, 128), BF16),
            dma((6 + chunks,)),
            dma((8,)),
            dma((8,)),
            dma((chunks * (1 + kernels),)),
            dma((chunks * (1 + kernels),)),
            dma((chunks * g.team,)),
            dma((chunks * g.team,)),
            dma((chunks * g.far,)),
            dma((chunks * g.far,)),
            dma((chunks * g.team,)),
            dma((chunks * g.team,)),
        ],
        compiler_params=pltpu.CompilerParams(
            collective_id=0, has_side_effects=True, vmem_limit_bytes=56 * 2**20
        ),
    )(
        cotangent.transpose(1, 0, 2),
        layer_input.transpose(1, 0, 2),
        weights.reshape(kernels * channels, channels),
        filter_values.transpose(0, 3, 2, 1),
        row_offset,
        reach,
    )
    shape = (kernels, channels, channels)
    input_grad, weight_grad = pl.pallas_call(
        functools.partial(deliver, 1.0 / math.sqrt(nlat * cols * lon)),
        out_shape=(jax.ShapeDtypeStruct(field, BF16), jax.ShapeDtypeStruct(shape, F32)),
        in_specs=[vmem, vmem],
        out_specs=(anywhere, anywhere),
        scratch_shapes=[pltpu.VMEM(shape, F32), dma((1 + kernels,))],
        compiler_params=pltpu.CompilerParams(vmem_limit_bytes=16 * 2**20),
    )(out, total)
    return input_grad.transpose(1, 0, 2), weight_grad


def solution(mesh):
    return jax.shard_map(
        on_device,
        mesh=mesh,
        in_specs=(P(None, "lat", "lon"), P(None, "lat", "lon"), P(), P(), P(), P()),
        out_specs=(P(None, "lat", "lon"), P()),
        check_vma=False,
    )
```

```python
import functools
import math

import jax
import jax.numpy as jnp
from jax import lax
from jax.experimental import pallas as pl
from jax.experimental.pallas import tpu as pltpu
from jax.sharding import PartitionSpec as P

MESH = pl.DeviceIdType.MESH
F32 = jnp.float32
BF16 = jnp.bfloat16


def iota(shape, dim):
    return lax.broadcasted_iota(jnp.int32, shape, dim)


def ceil_to(n, m):
    return -(-n // m) * m


class Plan:
    def __init__(self, lat, lon, channels, rows, cols, nlat, kernels, span, taps):
        self.lat, self.lon = lat, lon
        self.c, self.rows, self.cols = channels, rows, cols
        self.nlat, self.k, self.span, self.taps = nlat, kernels, span, taps
        self.q = (taps - 1) // 2
        self.rim = span - 1
        self.tall = rows + 2 * self.rim
        self.near = 2 * span - 1
        self.pairs = rows // 2
        self.window = self.near + 1
        self.band = self.window * cols
        self.deep = self.band + self.window * 16
        self.mix = kernels * channels
        self.z = lat // 4
        self.far = self.z // 2
        self.team = 4 * lon
        self.chunks = 2
        self.wide = channels // self.chunks
        self.slim = self.wide // 2
        self.tier = kernels * self.slim
        self.blocks = channels // 128
        self.half = self.blocks * self.tier
        self.piece = ceil_to(-(-self.half // self.team), 16)
        self.owners = self.half // self.piece
        self.idle = self.team - self.owners


def remote(src, dst, sems, n, device):
    return pltpu.make_async_remote_copy(
        src_ref=src,
        dst_ref=dst,
        send_sem=sems[0].at[n],
        recv_sem=sems[1].at[n],
        device_id=device,
        device_id_type=MESH,
    )


def kernel(
    g,
    cot,
    xin,
    w_in,
    fv_in,
    ro_in,
    reach_in,
    out,
    total_out,
    fv,
    ro,
    reach,
    cot_s,
    x_s,
    xt,
    w_s,
    wt,
    table,
    taps_s,
    toep,
    inner,
    sp,
    pack_l,
    pack_r,
    left,
    right,
    rim_s,
    rim_t,
    grad,
    core_in,
    grad16,
    team_in,
    far_in,
    final,
    local_sem,
    halo_send,
    halo_recv,
    core_send,
    core_recv,
    team_send,
    team_recv,
    far_send,
    far_recv,
    back_send,
    back_recv,
):
    lat = lax.axis_index("lat")
    lon = lax.axis_index("lon")
    core = lax.rem(lat, 2)
    zi = lax.rem(lat // 2, g.z)
    ylo = lat // (2 * g.z)
    z_lo, z_hi = lax.rem(zi, 2), zi // 2
    me = (ylo * g.lon + lon) * 2 + z_lo
    up, down = lax.rem(lat + 1, g.lat), lax.rem(lat + g.lat - 1, g.lat)
    east, west = lax.rem(lon + 1, g.lon), lax.rem(lon + g.lon - 1, g.lon)
    sibling = (lat + 1 - 2 * core, lon)

    def team_peer(d):
        peer = lax.rem(me + d, g.team)
        column = peer // 2
        z = 2 * z_hi + lax.rem(peer, 2)
        return peer, ((column // g.lon) * (2 * g.z) + 2 * z + core, lax.rem(column, g.lon))

    def far_peer(d):
        z = 2 * lax.rem(z_hi + d, g.far) + z_lo
        return (ylo * 2 * g.z + 2 * z + core, lon)

    halo = [
        (up, east),
        (up, west),
        (down, east),
        (down, west),
        (lat, east),
        (lat, west),
        (up, lon),
        (down, lon),
    ]
    partners = halo + [sibling]
    partners += [team_peer(d)[1] for d in range(1, g.team)]
    partners += [far_peer(d) for d in range(1, g.far)]

    barrier = pltpu.get_barrier_semaphore()
    for peer in partners:
        pl.semaphore_signal(barrier, inc=1, device_id=peer, device_id_type=MESH)

    load_cot = pltpu.make_async_copy(cot, cot_s.at[pl.ds(g.rim, g.rows)], local_sem.at[0])
    load_x = pltpu.make_async_copy(xin, x_s, local_sem.at[1])
    load_w = pltpu.make_async_copy(w_in, w_s, local_sem.at[2])
    load_taps = [
        pltpu.make_async_copy(source, target, local_sem.at[3 + g.chunks + n])
        for n, (source, target) in enumerate(((fv_in, fv), (ro_in, ro), (reach_in, reach)))
    ]
    load_cot.start()
    for copy in load_taps:
        copy.start()
    load_x.start()
    load_w.start()
    load_cot.wait()

    pick = iota((16, g.cols), 0)
    lane = iota((16, g.cols), 1)
    pick = (lane == jnp.where(pick < 8, pick + (g.cols - 8), pick - 8)).astype(F32).astype(BF16)
    for o in range(0, g.rows, 2):
        edge = [
            lax.dot_general(
                pick, cot_s[g.rim + o + n], (((1,), (1,)), ((), ())), preferred_element_type=F32
            )
            for n in range(2)
        ]
        pack_r[8 * o : 8 * o + 16, :] = jnp.concatenate([edge[0][:8], edge[1][:8]], 0).astype(BF16)
        pack_l[8 * o : 8 * o + 16, :] = jnp.concatenate([edge[0][8:], edge[1][8:]], 0).astype(BF16)

    pl.semaphore_wait(barrier, len(partners))

    sems = (halo_send, halo_recv)
    n_own = 8 * g.rows
    last = n_own - 32
    rim, tall, rows = g.rim, g.tall, g.rows
    sends = [
        remote(pack_r.at[pl.ds(last, 32)], left.at[pl.ds(0, 32)], sems, 0, halo[0]),
        remote(pack_l.at[pl.ds(last, 32)], right.at[pl.ds(0, 32)], sems, 1, halo[1]),
        remote(pack_r.at[pl.ds(0, 32)], left.at[pl.ds(32 + n_own, 32)], sems, 2, halo[2]),
        remote(pack_l.at[pl.ds(0, 32)], right.at[pl.ds(32 + n_own, 32)], sems, 3, halo[3]),
        remote(pack_r, left.at[pl.ds(32, n_own)], sems, 4, halo[4]),
        remote(pack_l, right.at[pl.ds(32, n_own)], sems, 5, halo[5]),
        remote(cot.at[pl.ds(rows - rim, rim)], cot_s.at[pl.ds(0, rim)], sems, 6, halo[6]),
        remote(cot.at[pl.ds(0, rim)], cot_s.at[pl.ds(tall - rim, rim)], sems, 7, halo[7]),
    ]
    for copy in sends:
        copy.start()

    for copy in load_taps:
        copy.wait()
    entries = g.k * g.taps * g.span
    for k in range(g.k):
        for t in range(g.taps):
            n = (k * g.taps + t) * g.span
            table[n : n + g.span, :] = fv[k, t].astype(F32)
    table[entries:, :] = jnp.zeros((256 - entries, g.nlat), F32)
    source = iota((32, g.nlat), 1)
    slot = iota((32, g.nlat), 0)
    here = (source == lat * rows - rim + slot) & (slot < tall)
    moved = lax.dot_general(
        here.astype(F32).astype(BF16),
        table[...].astype(BF16),
        (((1,), (1,)), ((), ())),
        preferred_element_type=F32,
    )
    first = jnp.where(here, ro[...].astype(F32)[None, :], 0.0)
    first = jnp.sum(first, axis=1, keepdims=True).astype(jnp.int32)
    reached = jnp.where(here, reach[...].astype(F32)[None, :], 0.0)
    reached = jnp.sum(reached, axis=1, keepdims=True).astype(jnp.int32)
    column = iota((32, 256), 1)
    level = column & 3
    order = column >> 2
    tap = order
    for n in range(1, g.k):
        tap = tap - jnp.where(order >= n * g.taps, g.taps, 0)
    moved = jnp.where(jnp.abs(tap - g.q) < reached, moved, 0.0)
    levels = jnp.concatenate(
        [jnp.where(level == g.rim - j - first, moved, 0.0) for j in range(g.near)], 0
    ).astype(BF16)
    entry = iota((256, g.k * 128), 0) >> 2
    place = iota((256, g.k * 128), 1)
    offset = ((place & 127) + g.q) & 127
    wanted = (place >> 7) * g.taps + offset
    spot = ((entry == wanted) & (offset < g.taps)).astype(F32).astype(BF16)
    placed = jnp.dot(levels, spot, preferred_element_type=F32)
    for k in range(g.k):
        taps_s[k] = placed[:, k * 128 : (k + 1) * 128]

    l_in = iota((g.cols, g.cols), 0)
    l_out = iota((g.cols, g.cols), 1)
    near = jnp.abs(l_in - l_out) <= g.q
    m_in = iota((8, g.cols), 0)
    m_out = iota((8, g.cols), 1)
    from_left = m_out <= m_in
    from_right = m_out >= m_in + (g.cols - 8)

    def build(p, carry):
        early = p < g.pairs // 2
        band = jnp.where(early, g.window * 16, 0)
        ends = jnp.where(early, 0, g.band)

        def band_at(at):
            return pl.ds(pl.multiple_of(band + at * 128, 128), 128)

        def ends_at(at):
            return pl.ds(pl.multiple_of(ends + at * 16, 16), 16)

        for i in range(2):
            empty = (g.window - 1) * (1 - i)
            for k in range(g.k):
                lanes = slice((2 * k + i) * 128, (2 * k + i + 1) * 128)
                toep[p, band_at(empty), lanes] = jnp.zeros((128, 128), BF16)
                toep[p, ends_at(empty), lanes] = jnp.zeros((16, 128), BF16)
                for j in range(g.near):
                    row = taps_s[k, pl.ds(j * 32 + 2 * p + i + j, 1), :]
                    wheel = pltpu.roll(
                        jnp.broadcast_to(row, (128, 128)), 0, 1, stride=1, stride_axis=0
                    )
                    at = i + j
                    toep[p, band_at(at), lanes] = jnp.where(near, wheel, 0.0).astype(BF16)
                    corner = jnp.concatenate(
                        [
                            jnp.where(from_left, wheel[120:], 0.0),
                            jnp.where(from_right, wheel[:8], 0.0),
                        ],
                        0,
                    )
                    toep[p, ends_at(at), lanes] = corner.astype(BF16)
        return carry

    lax.fori_loop(0, g.pairs, build, 0)

    def own_rows(p):
        return max(0, rim - 2 * p), min(g.window, rim + rows - 2 * p)

    for p in range(g.pairs):
        low, high = own_rows(p)
        start = g.window * 16 if p < g.pairs // 2 else 0
        wide = jnp.concatenate([cot_s[2 * p + j] for j in range(low, high)], 1)
        deep = toep[p, start + low * 128 : start + high * 128, :]
        inner[p] = jnp.dot(wide, deep, preferred_element_type=F32)

    load_x.wait()
    load_w.wait()
    for i in range(rows):
        xt[i * 128 : (i + 1) * 128, :] = x_s[i].T
    for k in range(g.k):
        wt[:, k * g.c : (k + 1) * g.c] = w_s[k * g.c : (k + 1) * g.c, :].T

    def lay_rim(w):
        at = 16 * ((w + 1) // 2)
        odd = 8 * ((w + 1) % 2)
        rim_s[16 * w : 16 * w + 16, :] = jnp.concatenate(
            [
                left[at : at + 16, :].astype(F32)[odd : odd + 8],
                right[at : at + 16, :].astype(F32)[odd : odd + 8],
            ],
            0,
        ).astype(BF16)

    def spread(p, part):
        low, high = own_rows(p)
        ends = rim_t[p, part, :]
        if p < g.pairs // 2:
            wide = [ends] + [cot_s[2 * p + j, part, :] for j in range(low)]
            deep = toep[p, : g.window * 16 + low * 128, :]
        else:
            wide = [cot_s[2 * p + j, part, :] for j in range(high, g.window)] + [ends]
            deep = toep[p, high * 128 :, :]
        total = jnp.dot(jnp.concatenate(wide, 1), deep, preferred_element_type=F32)
        total = total + inner[p, part, :]
        for k in range(g.k):
            at = slice(k * g.c + part.start, k * g.c + part.stop)
            sp[p, at, :] = total[:, k * 256 : (k + 1) * 256].astype(BF16)

    def turn(p):
        rim_t[p] = rim_s[32 * p : 32 * p + 16 * g.window, :].T

    whole = [p for p in range(g.pairs) if own_rows(p) == (0, g.window)]
    others = [p for p in range(g.pairs) if p not in whole]
    for n in (4, 5):
        sends[n].wait()
    for w in range(rim + 1, tall - rim - 1):
        lay_rim(w)
    for p in whole:
        turn(p)
        spread(p, slice(0, g.c))
    for n in (0, 1, 2, 3, 6, 7):
        sends[n].wait()
    for w in list(range(rim + 1)) + list(range(tall - rim - 1, tall)):
        lay_rim(w)

    def chunk(m):
        for p in others:
            if m == 0:
                turn(p)
            spread(p, slice(m * g.wide, (m + 1) * g.wide))

    def term(m, h):
        tiers = []
        for k in range(g.k):
            at = pl.multiple_of(k * g.c + m * g.wide + h * g.slim, 32)
            tiers.append(
                jnp.concatenate([sp[p, pl.ds(at, g.slim), :] for p in range(g.pairs)], 1)
            )
        return jnp.dot(jnp.concatenate(tiers, 0), xt[...], preferred_element_type=F32)

    to_core = [
        remote(grad.at[m], core_in.at[m], (core_send, core_recv), m, sibling)
        for m in range(g.chunks)
    ]

    def give(m):
        total = term(m, 1 - core)
        for b in range(g.blocks):
            grad[m, b * g.tier : (b + 1) * g.tier, :] = total[:, b * 128 : (b + 1) * 128]
        to_core[m].start()

    def keep(m):
        total = term(m, core)
        to_core[m].wait()
        for b in range(g.blocks):
            at = slice(b * g.tier, (b + 1) * g.tier)
            both = total[:, b * 128 : (b + 1) * 128] + core_in[m, at, :]
            grad16[m, at, :] = both.astype(BF16)

    def owned(index, m):
        n = index - m * g.idle
        return n, (n >= 0) & (n < g.owners)

    def rows_of(n):
        return pl.ds(pl.multiple_of(n * g.piece, 16), g.piece)

    def to_owner(m, d):
        peer, device = team_peer(d)
        n, valid = owned(peer, m)
        n = jnp.where(valid, n, 0)
        sems = (team_send, team_recv)
        at = team_in.at[m, d]
        return valid, remote(grad16.at[m, rows_of(n)], at, sems, m * g.team + d, device)

    def scatter(m):
        for d in range(1, g.team):
            valid, copy = to_owner(m, d)

            @pl.when(valid)
            def _():
                copy.start()

    def to_far(m, d):
        sems = (far_send, far_recv)
        here = far_in.at[m, z_hi]
        return remote(here, here, sems, m * g.far + d, far_peer(d))

    def add(m):
        n, mine = owned(me, m)

        @pl.when(mine)
        def _():
            total = grad16[m, rows_of(n), :].astype(F32)
            for d in range(1, g.team):
                to_owner(m, d)[1].wait_recv()
                total = total + team_in[m, d].astype(F32)
            far_in[m, z_hi] = total
            for d in range(1, g.far):
                to_far(m, d).start()

    def landing(m, n):
        b, r = n // (g.tier // g.piece), lax.rem(n, g.tier // g.piece)
        k, r = r // (g.slim // g.piece), lax.rem(r, g.slim // g.piece)
        row = k * g.c + m * g.wide + core * g.slim + r * g.piece
        return total_out.at[
            pl.ds(pl.multiple_of(row, 32), g.piece), pl.ds(pl.multiple_of(b * 128, 128), 128)
        ]

    def from_owner(m, d):
        there = landing(m, owned(me, m)[0])
        sems = (back_send, back_recv)
        return remote(final.at[m], there, sems, m * g.team + d, team_peer(d)[1])

    def lay_own(m):
        there = landing(m, owned(me, m)[0])
        return pltpu.make_async_copy(final.at[m], there, local_sem.at[3 + m])

    def finish(m):
        n, mine = owned(me, m)

        @pl.when(mine)
        def _():
            for d in range(1, g.far):
                to_far(m, d).wait()
            total = far_in[m, 0]
            for f in range(1, g.far):
                total = total + far_in[m, f]
            final[m] = total.astype(BF16)
            for d in range(1, g.team):
                from_owner(m, d).start()
            lay_own(m).start()

    def swap(m, k):
        row = pl.multiple_of(k * g.c + m * g.wide + core * g.slim, 32)
        block = total_out.at[pl.ds(row, g.slim)]
        sems = (core_send, core_recv)
        return remote(block, block, sems, g.chunks + m * g.k + k, sibling)

    def collect(m):
        _, mine = owned(me, m)
        for d in range(1, g.team):
            sender = lax.rem(me + g.team - d, g.team)
            n, valid = owned(sender, m)
            n = jnp.where(valid, n, 0)
            sems = (back_send, back_recv)
            copy = remote(final.at[m], landing(m, n), sems, m * g.team + d, team_peer(d)[1])

            @pl.when(valid)
            def _():
                copy.wait_recv()

        @pl.when(mine)
        def _():
            lay_own(m).wait()

        for k in range(g.k):
            swap(m, k).start()

    def drain(m):
        for d in range(1, g.team):
            valid, copy = to_owner(m, d)

            @pl.when(valid)
            def _():
                copy.wait_send()

        @pl.when(owned(me, m)[1])
        def _():
            for d in range(1, g.team):
                from_owner(m, d).wait_send()

    def inward(p, carry):
        total = jnp.dot(wt[...], sp[p], preferred_element_type=F32).astype(BF16)
        out[2 * p] = total[:, :128]
        out[2 * p + 1] = total[:, 128:]
        return carry

    chunk(0)
    give(0)
    chunk(1)
    give(1)
    keep(0)
    scatter(0)
    keep(1)
    scatter(1)
    lax.fori_loop(0, g.pairs, inward, 0)
    add(0)
    add(1)
    finish(0)
    finish(1)
    collect(0)
    collect(1)
    for m in range(g.chunks):
        drain(m)
    for m in range(g.chunks):
        for k in range(g.k):
            swap(m, k).wait()


def deliver(scale, field, total, out, weight_grad, wide, sems):
    store = [pltpu.make_async_copy(field, out, sems.at[0])]
    store[0].start()
    kernels, channels, _ = wide.shape
    for k in range(kernels):
        wide[k] = total[k * channels : (k + 1) * channels, :].astype(F32) * scale
        store.append(pltpu.make_async_copy(wide.at[k], weight_grad.at[k], sems.at[1 + k]))
        store[-1].start()
    for copy in store:
        copy.wait()


def on_device(cotangent, layer_input, filter_values, weights, row_offset, reach):
    channels, rows, cols = cotangent.shape
    kernels, nlat, span, taps = filter_values.shape
    lat, lon = lax.axis_size("lat"), lax.axis_size("lon")
    g = Plan(lat, lon, channels, rows, cols, nlat, kernels, span, taps)
    anywhere = pl.BlockSpec(memory_space=pl.ANY)
    vmem = pl.BlockSpec(memory_space=pltpu.VMEM)
    dma = pltpu.SemaphoreType.DMA
    field = (rows, channels, cols)
    chunks = g.chunks
    out, total = pl.pallas_call(
        functools.partial(kernel, g),
        out_shape=(
            pltpu.VMEM(field, BF16),
            pltpu.VMEM((g.mix, channels), BF16),
        ),
        in_specs=[anywhere] * 6,
        out_specs=(vmem, vmem),
        scratch_shapes=[
            pltpu.VMEM((kernels, taps, span, nlat), BF16),
            pltpu.VMEM((nlat,), jnp.int32),
            pltpu.VMEM((nlat,), jnp.int32),
            pltpu.VMEM((g.tall, channels, cols), BF16),
            pltpu.VMEM(field, BF16),
            pltpu.VMEM((rows * cols, channels), BF16),
            pltpu.VMEM((g.mix, channels), BF16),
            pltpu.VMEM((channels, g.mix), BF16),
            pltpu.VMEM((256, nlat), F32),
            pltpu.VMEM((kernels, g.near * 32, 128), F32),
            pltpu.VMEM((g.pairs, g.deep, kernels * 256), BF16),
            pltpu.VMEM((g.pairs, channels, kernels * 256), F32),
            pltpu.VMEM((g.pairs, g.mix, 256), BF16),
            pltpu.VMEM((8 * rows, channels), BF16),
            pltpu.VMEM((8 * rows, channels), BF16),
            pltpu.VMEM((8 * rows + 64, channels), BF16),
            pltpu.VMEM((8 * rows + 64, channels), BF16),
            pltpu.VMEM((16 * g.tall, channels), BF16),
            pltpu.VMEM((g.pairs, channels, 128), BF16),
            pltpu.VMEM((chunks, g.half, 128), F32),
            pltpu.VMEM((chunks, g.half, 128), F32),
            pltpu.VMEM((chunks, g.half, 128), BF16),
            pltpu.VMEM((chunks, g.team, g.piece, 128), BF16),
            pltpu.VMEM((chunks, g.far, g.piece, 128), F32),
            pltpu.VMEM((chunks, g.piece, 128), BF16),
            dma((6 + chunks,)),
            dma((8,)),
            dma((8,)),
            dma((chunks * (1 + kernels),)),
            dma((chunks * (1 + kernels),)),
            dma((chunks * g.team,)),
            dma((chunks * g.team,)),
            dma((chunks * g.far,)),
            dma((chunks * g.far,)),
            dma((chunks * g.team,)),
            dma((chunks * g.team,)),
        ],
        compiler_params=pltpu.CompilerParams(
            collective_id=0, has_side_effects=True, vmem_limit_bytes=56 * 2**20
        ),
    )(
        cotangent.transpose(1, 0, 2),
        layer_input.transpose(1, 0, 2),
        weights.reshape(kernels * channels, channels),
        filter_values.transpose(0, 3, 2, 1),
        row_offset,
        reach,
    )
    shape = (kernels, channels, channels)
    input_grad, weight_grad = pl.pallas_call(
        functools.partial(deliver, 1.0 / math.sqrt(nlat * cols * lon)),
        out_shape=(jax.ShapeDtypeStruct(field, BF16), jax.ShapeDtypeStruct(shape, F32)),
        in_specs=[vmem, vmem],
        out_specs=(anywhere, anywhere),
        scratch_shapes=[pltpu.VMEM(shape, F32), dma((1 + kernels,))],
        compiler_params=pltpu.CompilerParams(vmem_limit_bytes=16 * 2**20),
    )(out, total)
    return input_grad.transpose(1, 0, 2), weight_grad


def solution(mesh):
    return jax.shard_map(
        on_device,
        mesh=mesh,
        in_specs=(P(None, "lat", "lon"), P(None, "lat", "lon"), P(), P(), P(), P()),
        out_specs=(P(None, "lat", "lon"), P()),
        check_vma=False,
    )
```

```python
import functools
import math

import jax
import jax.numpy as jnp
from jax import lax
from jax.experimental import pallas as pl
from jax.experimental.pallas import tpu as pltpu
from jax.sharding import PartitionSpec as P

MESH = pl.DeviceIdType.MESH
F32 = jnp.float32
BF16 = jnp.bfloat16


def iota(shape, dim):
    return lax.broadcasted_iota(jnp.int32, shape, dim)


def ceil_to(n, m):
    return -(-n // m) * m


class Plan:
    def __init__(self, lat, lon, channels, rows, cols, nlat, kernels, span, taps):
        self.lat, self.lon = lat, lon
        self.c, self.rows, self.cols = channels, rows, cols
        self.nlat, self.k, self.span, self.taps = nlat, kernels, span, taps
        self.q = (taps - 1) // 2
        self.rim = span - 1
        self.tall = rows + 2 * self.rim
        self.near = 2 * span - 1
        self.pairs = rows // 2
        self.window = self.near + 1
        self.band = self.window * cols
        self.deep = self.band + self.window * 16
        self.mix = kernels * channels
        self.z = lat // 4
        self.far = self.z // 2
        self.team = 4 * lon
        self.chunks = 2
        self.wide = channels // self.chunks
        self.slim = self.wide // 2
        self.tier = kernels * self.slim
        self.blocks = channels // 128
        self.half = self.blocks * self.tier
        self.piece = ceil_to(-(-self.half // self.team), 16)
        self.owners = self.half // self.piece
        self.idle = self.team - self.owners


def remote(src, dst, sems, n, device):
    return pltpu.make_async_remote_copy(
        src_ref=src,
        dst_ref=dst,
        send_sem=sems[0].at[n],
        recv_sem=sems[1].at[n],
        device_id=device,
        device_id_type=MESH,
    )


def kernel(
    g,
    cot,
    xin,
    w_in,
    fv_in,
    ro_in,
    reach_in,
    out,
    total_out,
    fv,
    ro,
    reach,
    cot_s,
    x_s,
    xt,
    w_s,
    wt,
    table,
    taps_s,
    toep,
    inner,
    sp,
    pack_l,
    pack_r,
    left,
    right,
    rim_s,
    rim_t,
    grad,
    core_in,
    grad16,
    team_in,
    far_in,
    final,
    local_sem,
    halo_send,
    halo_recv,
    core_send,
    core_recv,
    team_send,
    team_recv,
    far_send,
    far_recv,
    back_send,
    back_recv,
):
    lat = lax.axis_index("lat")
    lon = lax.axis_index("lon")
    core = lax.rem(lat, 2)
    zi = lax.rem(lat // 2, g.z)
    ylo = lat // (2 * g.z)
    z_lo, z_hi = lax.rem(zi, 2), zi // 2
    me = (ylo * g.lon + lon) * 2 + z_lo
    up, down = lax.rem(lat + 1, g.lat), lax.rem(lat + g.lat - 1, g.lat)
    east, west = lax.rem(lon + 1, g.lon), lax.rem(lon + g.lon - 1, g.lon)
    sibling = (lat + 1 - 2 * core, lon)

    def team_peer(d):
        peer = lax.rem(me + d, g.team)
        column = peer // 2
        z = 2 * z_hi + lax.rem(peer, 2)
        return peer, ((column // g.lon) * (2 * g.z) + 2 * z + core, lax.rem(column, g.lon))

    def far_peer(d):
        z = 2 * lax.rem(z_hi + d, g.far) + z_lo
        return (ylo * 2 * g.z + 2 * z + core, lon)

    halo = [
        (up, east),
        (up, west),
        (down, east),
        (down, west),
        (lat, east),
        (lat, west),
        (up, lon),
        (down, lon),
    ]
    partners = halo + [sibling]
    partners += [team_peer(d)[1] for d in range(1, g.team)]
    partners += [far_peer(d) for d in range(1, g.far)]

    barrier = pltpu.get_barrier_semaphore()
    for peer in partners:
        pl.semaphore_signal(barrier, inc=1, device_id=peer, device_id_type=MESH)

    load_cot = pltpu.make_async_copy(cot, cot_s.at[pl.ds(g.rim, g.rows)], local_sem.at[0])
    load_x = pltpu.make_async_copy(xin, x_s, local_sem.at[1])
    load_w = pltpu.make_async_copy(w_in, w_s, local_sem.at[2])
    load_taps = [
        pltpu.make_async_copy(source, target, local_sem.at[3 + g.chunks + n])
        for n, (source, target) in enumerate(((fv_in, fv), (ro_in, ro), (reach_in, reach)))
    ]
    load_cot.start()
    for copy in load_taps:
        copy.start()
    load_x.start()
    load_w.start()
    load_cot.wait()

    pick = iota((16, g.cols), 0)
    lane = iota((16, g.cols), 1)
    pick = (lane == jnp.where(pick < 8, pick + (g.cols - 8), pick - 8)).astype(F32).astype(BF16)
    for o in range(0, g.rows, 2):
        edge = [
            lax.dot_general(
                pick, cot_s[g.rim + o + n], (((1,), (1,)), ((), ())), preferred_element_type=F32
            )
            for n in range(2)
        ]
        pack_r[8 * o : 8 * o + 16, :] = jnp.concatenate([edge[0][:8], edge[1][:8]], 0).astype(BF16)
        pack_l[8 * o : 8 * o + 16, :] = jnp.concatenate([edge[0][8:], edge[1][8:]], 0).astype(BF16)

    pl.semaphore_wait(barrier, len(partners))

    sems = (halo_send, halo_recv)
    n_own = 8 * g.rows
    last = n_own - 32
    rim, tall, rows = g.rim, g.tall, g.rows
    sends = [
        remote(pack_r.at[pl.ds(last, 32)], left.at[pl.ds(0, 32)], sems, 0, halo[0]),
        remote(pack_l.at[pl.ds(last, 32)], right.at[pl.ds(0, 32)], sems, 1, halo[1]),
        remote(pack_r.at[pl.ds(0, 32)], left.at[pl.ds(32 + n_own, 32)], sems, 2, halo[2]),
        remote(pack_l.at[pl.ds(0, 32)], right.at[pl.ds(32 + n_own, 32)], sems, 3, halo[3]),
        remote(pack_r, left.at[pl.ds(32, n_own)], sems, 4, halo[4]),
        remote(pack_l, right.at[pl.ds(32, n_own)], sems, 5, halo[5]),
        remote(cot.at[pl.ds(rows - rim, rim)], cot_s.at[pl.ds(0, rim)], sems, 6, halo[6]),
        remote(cot.at[pl.ds(0, rim)], cot_s.at[pl.ds(tall - rim, rim)], sems, 7, halo[7]),
    ]
    for copy in sends:
        copy.start()

    for copy in load_taps:
        copy.wait()
    entries = g.k * g.taps * g.span
    for k in range(g.k):
        for t in range(g.taps):
            n = (k * g.taps + t) * g.span
            table[n : n + g.span, :] = fv[k, t].astype(F32)
    table[entries:, :] = jnp.zeros((256 - entries, g.nlat), F32)
    source = iota((32, g.nlat), 1)
    slot = iota((32, g.nlat), 0)
    here = (source == lat * rows - rim + slot) & (slot < tall)
    moved = lax.dot_general(
        here.astype(F32).astype(BF16),
        table[...].astype(BF16),
        (((1,), (1,)), ((), ())),
        preferred_element_type=F32,
    )
    first = jnp.where(here, ro[...].astype(F32)[None, :], 0.0)
    first = jnp.sum(first, axis=1, keepdims=True).astype(jnp.int32)
    reached = jnp.where(here, reach[...].astype(F32)[None, :], 0.0)
    reached = jnp.sum(reached, axis=1, keepdims=True).astype(jnp.int32)
    column = iota((32, 256), 1)
    level = column & 3
    order = column >> 2
    tap = order
    for n in range(1, g.k):
        tap = tap - jnp.where(order >= n * g.taps, g.taps, 0)
    moved = jnp.where(jnp.abs(tap - g.q) < reached, moved, 0.0)
    levels = jnp.concatenate(
        [jnp.where(level == g.rim - j - first, moved, 0.0) for j in range(g.near)], 0
    ).astype(BF16)
    entry = iota((256, g.k * 128), 0) >> 2
    place = iota((256, g.k * 128), 1)
    offset = ((place & 127) + g.q) & 127
    wanted = (place >> 7) * g.taps + offset
    spot = ((entry == wanted) & (offset < g.taps)).astype(F32).astype(BF16)
    placed = jnp.dot(levels, spot, preferred_element_type=F32)
    for k in range(g.k):
        taps_s[k] = placed[:, k * 128 : (k + 1) * 128]

    l_in = iota((g.cols, g.cols), 0)
    l_out = iota((g.cols, g.cols), 1)
    near = jnp.abs(l_in - l_out) <= g.q
    m_in = iota((8, g.cols), 0)
    m_out = iota((8, g.cols), 1)
    from_left = m_out <= m_in
    from_right = m_out >= m_in + (g.cols - 8)

    def build(p, carry):
        early = p < g.pairs // 2
        band = jnp.where(early, g.window * 16, 0)
        ends = jnp.where(early, 0, g.band)

        def band_at(at):
            return pl.ds(pl.multiple_of(band + at * 128, 128), 128)

        def ends_at(at):
            return pl.ds(pl.multiple_of(ends + at * 16, 16), 16)

        for i in range(2):
            empty = (g.window - 1) * (1 - i)
            for k in range(g.k):
                lanes = slice((2 * k + i) * 128, (2 * k + i + 1) * 128)
                toep[p, band_at(empty), lanes] = jnp.zeros((128, 128), BF16)
                toep[p, ends_at(empty), lanes] = jnp.zeros((16, 128), BF16)
                for j in range(g.near):
                    row = taps_s[k, pl.ds(j * 32 + 2 * p + i + j, 1), :]
                    wheel = pltpu.roll(
                        jnp.broadcast_to(row, (128, 128)), 0, 1, stride=1, stride_axis=0
                    )
                    at = i + j
                    toep[p, band_at(at), lanes] = jnp.where(near, wheel, 0.0).astype(BF16)
                    corner = jnp.concatenate(
                        [
                            jnp.where(from_left, wheel[120:], 0.0),
                            jnp.where(from_right, wheel[:8], 0.0),
                        ],
                        0,
                    )
                    toep[p, ends_at(at), lanes] = corner.astype(BF16)
        return carry

    lax.fori_loop(0, g.pairs, build, 0)

    def own_rows(p):
        return max(0, rim - 2 * p), min(g.window, rim + rows - 2 * p)

    for p in range(g.pairs):
        low, high = own_rows(p)
        start = g.window * 16 if p < g.pairs // 2 else 0
        wide = jnp.concatenate([cot_s[2 * p + j] for j in range(low, high)], 1)
        deep = toep[p, start + low * 128 : start + high * 128, :]
        inner[p] = jnp.dot(wide, deep, preferred_element_type=F32)

    load_x.wait()
    for i in range(rows):
        xt[i * 128 : (i + 1) * 128, :] = x_s[i].T

    def lay_rim(w):
        at = 16 * ((w + 1) // 2)
        odd = 8 * ((w + 1) % 2)
        rim_s[16 * w : 16 * w + 16, :] = jnp.concatenate(
            [
                left[at : at + 16, :].astype(F32)[odd : odd + 8],
                right[at : at + 16, :].astype(F32)[odd : odd + 8],
            ],
            0,
        ).astype(BF16)

    def spread(p, part):
        low, high = own_rows(p)
        ends = rim_t[p, part, :]
        if p < g.pairs // 2:
            wide = [ends] + [cot_s[2 * p + j, part, :] for j in range(low)]
            deep = toep[p, : g.window * 16 + low * 128, :]
        else:
            wide = [cot_s[2 * p + j, part, :] for j in range(high, g.window)] + [ends]
            deep = toep[p, high * 128 :, :]
        total = jnp.dot(jnp.concatenate(wide, 1), deep, preferred_element_type=F32)
        total = total + inner[p, part, :]
        for k in range(g.k):
            at = slice(k * g.c + part.start, k * g.c + part.stop)
            sp[p, at, :] = total[:, k * 256 : (k + 1) * 256].astype(BF16)

    def turn(p):
        rim_t[p] = rim_s[32 * p : 32 * p + 16 * g.window, :].T

    whole = [p for p in range(g.pairs) if own_rows(p) == (0, g.window)]
    others = [p for p in range(g.pairs) if p not in whole]
    for n in (4, 5):
        sends[n].wait()
    for w in range(rim + 1, tall - rim - 1):
        lay_rim(w)
    for p in whole:
        turn(p)
        spread(p, slice(0, g.c))
    for n in (0, 1, 2, 3, 6, 7):
        sends[n].wait()
    for w in list(range(rim + 1)) + list(range(tall - rim - 1, tall)):
        lay_rim(w)

    def chunk(m):
        for p in others:
            if m == 0:
                turn(p)
            spread(p, slice(m * g.wide, (m + 1) * g.wide))

    def term(m, h):
        tiers = []
        for k in range(g.k):
            at = pl.multiple_of(k * g.c + m * g.wide + h * g.slim, 32)
            tiers.append(
                jnp.concatenate([sp[p, pl.ds(at, g.slim), :] for p in range(g.pairs)], 1)
            )
        return jnp.dot(jnp.concatenate(tiers, 0), xt[...], preferred_element_type=F32)

    to_core = [
        remote(grad.at[m], core_in.at[m], (core_send, core_recv), m, sibling)
        for m in range(g.chunks)
    ]

    def give(m):
        total = term(m, 1 - core)
        for b in range(g.blocks):
            grad[m, b * g.tier : (b + 1) * g.tier, :] = total[:, b * 128 : (b + 1) * 128]
        to_core[m].start()

    def keep(m):
        total = term(m, core)
        to_core[m].wait()
        for b in range(g.blocks):
            at = slice(b * g.tier, (b + 1) * g.tier)
            both = total[:, b * 128 : (b + 1) * 128] + core_in[m, at, :]
            grad16[m, at, :] = both.astype(BF16)

    def owned(index, m):
        n = index - m * g.idle
        return n, (n >= 0) & (n < g.owners)

    def rows_of(n):
        return pl.ds(pl.multiple_of(n * g.piece, 16), g.piece)

    def to_owner(m, d):
        peer, device = team_peer(d)
        n, valid = owned(peer, m)
        n = jnp.where(valid, n, 0)
        sems = (team_send, team_recv)
        at = team_in.at[m, d]
        return valid, remote(grad16.at[m, rows_of(n)], at, sems, m * g.team + d, device)

    def scatter(m):
        for d in range(1, g.team):
            valid, copy = to_owner(m, d)

            @pl.when(valid)
            def _():
                copy.start()

    def to_far(m, d):
        sems = (far_send, far_recv)
        here = far_in.at[m, z_hi]
        return remote(here, here, sems, m * g.far + d, far_peer(d))

    def add(m):
        n, mine = owned(me, m)

        @pl.when(mine)
        def _():
            total = grad16[m, rows_of(n), :].astype(F32)
            for d in range(1, g.team):
                to_owner(m, d)[1].wait_recv()
                total = total + team_in[m, d].astype(F32)
            far_in[m, z_hi] = total
            for d in range(1, g.far):
                to_far(m, d).start()

    def landing(m, n):
        b, r = n // (g.tier // g.piece), lax.rem(n, g.tier // g.piece)
        k, r = r // (g.slim // g.piece), lax.rem(r, g.slim // g.piece)
        row = k * g.c + m * g.wide + core * g.slim + r * g.piece
        return total_out.at[
            pl.ds(pl.multiple_of(row, 32), g.piece), pl.ds(pl.multiple_of(b * 128, 128), 128)
        ]

    def from_owner(m, d):
        there = landing(m, owned(me, m)[0])
        sems = (back_send, back_recv)
        return remote(final.at[m], there, sems, m * g.team + d, team_peer(d)[1])

    def lay_own(m):
        there = landing(m, owned(me, m)[0])
        return pltpu.make_async_copy(final.at[m], there, local_sem.at[3 + m])

    def finish(m):
        n, mine = owned(me, m)

        @pl.when(mine)
        def _():
            for d in range(1, g.far):
                to_far(m, d).wait()
            total = far_in[m, 0]
            for f in range(1, g.far):
                total = total + far_in[m, f]
            final[m] = total.astype(BF16)
            for d in range(1, g.team):
                from_owner(m, d).start()
            lay_own(m).start()

    def swap(m, k):
        row = pl.multiple_of(k * g.c + m * g.wide + core * g.slim, 32)
        block = total_out.at[pl.ds(row, g.slim)]
        sems = (core_send, core_recv)
        return remote(block, block, sems, g.chunks + m * g.k + k, sibling)

    def collect(m):
        _, mine = owned(me, m)
        for d in range(1, g.team):
            sender = lax.rem(me + g.team - d, g.team)
            n, valid = owned(sender, m)
            n = jnp.where(valid, n, 0)
            sems = (back_send, back_recv)
            copy = remote(final.at[m], landing(m, n), sems, m * g.team + d, team_peer(d)[1])

            @pl.when(valid)
            def _():
                copy.wait_recv()

        @pl.when(mine)
        def _():
            lay_own(m).wait()

        for k in range(g.k):
            swap(m, k).start()

    def drain(m):
        for d in range(1, g.team):
            valid, copy = to_owner(m, d)

            @pl.when(valid)
            def _():
                copy.wait_send()

        @pl.when(owned(me, m)[1])
        def _():
            for d in range(1, g.team):
                from_owner(m, d).wait_send()

    def inward(p, carry):
        total = jnp.dot(wt[...], sp[p], preferred_element_type=F32).astype(BF16)
        out[2 * p] = total[:, :128]
        out[2 * p + 1] = total[:, 128:]
        return carry

    chunk(0)
    give(0)
    chunk(1)
    give(1)
    keep(0)
    scatter(0)
    keep(1)
    scatter(1)
    load_w.wait()
    for k in range(g.k):
        wt[:, k * g.c : (k + 1) * g.c] = w_s[k * g.c : (k + 1) * g.c, :].T
    lax.fori_loop(0, g.pairs, inward, 0)
    add(0)
    add(1)
    finish(0)
    finish(1)
    collect(0)
    collect(1)
    for m in range(g.chunks):
        drain(m)
    for m in range(g.chunks):
        for k in range(g.k):
            swap(m, k).wait()


def deliver(scale, field, total, out, weight_grad, wide, sems):
    store = [pltpu.make_async_copy(field, out, sems.at[0])]
    store[0].start()
    kernels, channels, _ = wide.shape
    for k in range(kernels):
        wide[k] = total[k * channels : (k + 1) * channels, :].astype(F32) * scale
        store.append(pltpu.make_async_copy(wide.at[k], weight_grad.at[k], sems.at[1 + k]))
        store[-1].start()
    for copy in store:
        copy.wait()


def on_device(cotangent, layer_input, filter_values, weights, row_offset, reach):
    channels, rows, cols = cotangent.shape
    kernels, nlat, span, taps = filter_values.shape
    lat, lon = lax.axis_size("lat"), lax.axis_size("lon")
    g = Plan(lat, lon, channels, rows, cols, nlat, kernels, span, taps)
    anywhere = pl.BlockSpec(memory_space=pl.ANY)
    vmem = pl.BlockSpec(memory_space=pltpu.VMEM)
    dma = pltpu.SemaphoreType.DMA
    field = (rows, channels, cols)
    chunks = g.chunks
    out, total = pl.pallas_call(
        functools.partial(kernel, g),
        out_shape=(
            pltpu.VMEM(field, BF16),
            pltpu.VMEM((g.mix, channels), BF16),
        ),
        in_specs=[anywhere] * 6,
        out_specs=(vmem, vmem),
        scratch_shapes=[
            pltpu.VMEM((kernels, taps, span, nlat), BF16),
            pltpu.VMEM((nlat,), jnp.int32),
            pltpu.VMEM((nlat,), jnp.int32),
            pltpu.VMEM((g.tall, channels, cols), BF16),
            pltpu.VMEM(field, BF16),
            pltpu.VMEM((rows * cols, channels), BF16),
            pltpu.VMEM((g.mix, channels), BF16),
            pltpu.VMEM((channels, g.mix), BF16),
            pltpu.VMEM((256, nlat), F32),
            pltpu.VMEM((kernels, g.near * 32, 128), F32),
            pltpu.VMEM((g.pairs, g.deep, kernels * 256), BF16),
            pltpu.VMEM((g.pairs, channels, kernels * 256), F32),
            pltpu.VMEM((g.pairs, g.mix, 256), BF16),
            pltpu.VMEM((8 * rows, channels), BF16),
            pltpu.VMEM((8 * rows, channels), BF16),
            pltpu.VMEM((8 * rows + 64, channels), BF16),
            pltpu.VMEM((8 * rows + 64, channels), BF16),
            pltpu.VMEM((16 * g.tall, channels), BF16),
            pltpu.VMEM((g.pairs, channels, 128), BF16),
            pltpu.VMEM((chunks, g.half, 128), F32),
            pltpu.VMEM((chunks, g.half, 128), F32),
            pltpu.VMEM((chunks, g.half, 128), BF16),
            pltpu.VMEM((chunks, g.team, g.piece, 128), BF16),
            pltpu.VMEM((chunks, g.far, g.piece, 128), F32),
            pltpu.VMEM((chunks, g.piece, 128), BF16),
            dma((6 + chunks,)),
            dma((8,)),
            dma((8,)),
            dma((chunks * (1 + kernels),)),
            dma((chunks * (1 + kernels),)),
            dma((chunks * g.team,)),
            dma((chunks * g.team,)),
            dma((chunks * g.far,)),
            dma((chunks * g.far,)),
            dma((chunks * g.team,)),
            dma((chunks * g.team,)),
        ],
        compiler_params=pltpu.CompilerParams(
            collective_id=0, has_side_effects=True, vmem_limit_bytes=56 * 2**20
        ),
    )(
        cotangent.transpose(1, 0, 2),
        layer_input.transpose(1, 0, 2),
        weights.reshape(kernels * channels, channels),
        filter_values.transpose(0, 3, 2, 1),
        row_offset,
        reach,
    )
    shape = (kernels, channels, channels)
    input_grad, weight_grad = pl.pallas_call(
        functools.partial(deliver, 1.0 / math.sqrt(nlat * cols * lon)),
        out_shape=(jax.ShapeDtypeStruct(field, BF16), jax.ShapeDtypeStruct(shape, F32)),
        in_specs=[vmem, vmem],
        out_specs=(anywhere, anywhere),
        scratch_shapes=[pltpu.VMEM(shape, F32), dma((1 + kernels,))],
        compiler_params=pltpu.CompilerParams(vmem_limit_bytes=16 * 2**20),
    )(out, total)
    return input_grad.transpose(1, 0, 2), weight_grad


def solution(mesh):
    return jax.shard_map(
        on_device,
        mesh=mesh,
        in_specs=(P(None, "lat", "lon"), P(None, "lat", "lon"), P(), P(), P(), P()),
        out_specs=(P(None, "lat", "lon"), P()),
        check_vma=False,
    )
```
